512 devices in a mesh: grp: 16 (over z), dev: 32 (over x, y, core).
Axes of the slice: x: 4, y: 4, z: 16, core: 2. Of those that a mesh axis runs over, the one named last changes fastest.
Arguments:
- elem_stiff: bfloat16 [576, 1048576], P(None, ('grp', 'dev')), as said below
- density: float32 [1048576], P(('grp', 'dev')), may hold values from 0.05 to 1
- owner: int32 [131072, 1], P(('grp', 'dev')), may hold values from 0 to 31; in each aligned block of 256 rows (0 to 255, 256 to 511, ...) at most 16 rows name the same one
- agg_slot: int32 [131072], P(('grp', 'dev')), may hold values from 0 to 63
- par_octant: int32 [131072], P(('grp', 'dev')), may hold values from 0 to 7
- agg_octant: int32 [32768], P(('grp', 'dev')), may hold values from 0 to 7
- coarse_map: int32 [32768], P(('grp', 'dev')), may hold values from 0 to 15
Outputs:
- level_two: float32 [576, 32768], P(None, ('grp', 'dev'))
- coarse: float32 [576, 512], P(None, 'dev')
The draws below stay inside these ranges and needn't reach their ends.
Inputs may be any that keep to these rules, and one draw needn't show every extreme that they name: Among the parents of one device no owner is named more than 16 times, a bound that some block reaches. `elem_stiff`: every element matrix is symmetric.
All inputs are finite; a program needn't handle non-finite values.
Results may differ from the reference program's by a relative error of at most 0.0003.
Values sent between devices are 32-bit elements; how exact they have to be, the bound alone decides.
A program may use at most 128 MiB of HBM per device.

```python
import math
import jax
import jax.numpy as jnp
import numpy as np
from jax import lax

ELEM_DEV = 2048
PAR_DEV = 256
AGG_DEV = 64
COARSE_DEV = 16
CAP = 16
ELEMS = 1048576
PARENTS = 131072
AGGS = 32768
N_GRP = 16
N_DEV = 32


def build_stiff(key, half_width, bias, diag_lo, diag_hi, spread):
    key_off, key_diag, key_scale = jax.random.split(key, 3)
    off = jax.random.uniform(key_off, (24, 24, ELEMS), jnp.float32, -half_width, half_width)
    diag = jax.random.uniform(key_diag, (24, ELEMS), jnp.float32, diag_lo, diag_hi)
    scale = jnp.exp(jax.random.uniform(key_scale, (ELEMS,), jnp.float32, -spread, spread))
    index = jnp.arange(24, dtype=jnp.int32)
    same = (index[:, None] % 3 == index[None, :] % 3).astype(jnp.float32)[:, :, None]
    eye = jnp.eye(24, dtype=jnp.float32)[:, :, None]
    sym = off + jnp.transpose(off, (1, 0, 2)) + bias * same
    mats = sym * (1.0 - eye) + eye * diag[:, None, :]
    return (mats * scale[None, None, :]).reshape(576, ELEMS)


def draw_elem_stiff(key, part):
    key = jax.random.fold_in(key, 11)
    return build_stiff(key, 0.25, -0.2, 2.8, 3.6, 0.4).astype(jnp.bfloat16)


def place_ends(array, own_key, low, largest):
    index_at = [jax.random.randint(jax.random.fold_in(own_key, axis), (), 0, length) for axis, length in enumerate(array.shape)]
    widest = array.shape.index(max(array.shape))
    beside = index_at[:widest] + [(index_at[widest] + 1) % array.shape[widest]] + index_at[widest + 1:]
    return array.at[tuple(index_at)].set(low).at[tuple(beside)].set(largest)


def level_of(rng, dims, cuts, low, high):
    def one(dim, shards_of):
        draws = jax.random.uniform(jax.random.fold_in(jax.random.fold_in(rng, 6), dim), (shards_of,), jnp.float32, low / len(cuts), high / len(cuts))
        return jnp.repeat(jnp.exp(draws), dims[dim] // shards_of).reshape((-1,) + (1,) * (len(dims) - dim - 1))

    level = one(*cuts[0])
    for cut in cuts[1:]:
        level = level * one(*cut)
    return level


def routed_block(stream_key, own, number, rows, number_of, top, bound, skew):
    sequence = jax.random.permutation(stream_key, number_of)
    packed, common = shares(number_of, rows * top, bound, skew, True), shares(number_of, rows * top, bound, skew, False)
    places = jnp.arange(number_of)

    def named(tallies, rotation):
        used = int((tallies > 0).sum())
        fixed = max(1, used // 4)
        shifted = fixed + (places - fixed + rotation * (used - fixed)) % max(1, number_of - fixed)
        return jnp.zeros((number_of,), jnp.int32).at[sequence[jnp.where(places < fixed, places, shifted)]].set(jnp.asarray(tallies, jnp.int32))

    tallies = jnp.where(number % 4 == 0, named(packed, number // 4), named(common, number - number // 4 - 1))
    mixed = jax.random.permutation(jax.random.fold_in(own, 3), number_of)
    source_of, taker = mixed[0:number_of // 2 * 2:2], mixed[1:number_of // 2 * 2:2]
    room = jnp.minimum(tallies[source_of] - 1, bound - tallies[taker]) // 2
    room = jnp.where((source_of == sequence[0]) | (taker == sequence[0]) | (tallies[taker] == 0), 0, jnp.maximum(room, 0))
    shifted = jax.random.randint(jax.random.fold_in(own, 4), (number_of // 2,), 0, 1 << 20) % (room + 1)
    tallies = tallies.at[source_of].add(-shifted).at[taker].add(shifted)
    items = jnp.searchsorted(jnp.cumsum(tallies), jnp.arange(rows * top), side="right").astype(jnp.int32)
    listing = items.reshape(top, rows).T
    listing = listing[jax.random.permutation(jax.random.fold_in(own, 1), rows)]
    rotation = jax.random.randint(jax.random.fold_in(own, 2), (rows, 1), 0, top)
    return jnp.take_along_axis(listing, (jnp.arange(top)[None, :] + rotation) % top, axis=1)


def shares(count, total, reach, slope, full):
    weights = [(1 << 20) // math.isqrt(standing ** slope) + 1 for standing in range(1, count + 1)]
    largest = reach if full else min(reach, max(-(-total // count), total * weights[0] // sum(weights)))
    least = 1 if total - largest >= count - 1 else 0
    given, surplus = [largest] + [least] * (count - 1), total - largest - least * (count - 1)
    while surplus > 0:
        free = [i for i in range(1, count) if given[i] < largest] or [i for i in range(1, count) if given[i] < reach]
        whole, budget = sum([weights[i] for i in free]), surplus
        for i in free:
            extra = min(reach - given[i], max(1, budget * weights[i] // whole), surplus)
            given[i] = given[i] + extra
            surplus = surplus - extra
    return np.array(given)


def setup_inputs(seed: int = 0) -> dict:
    seeds = jax.random.split(jax.random.key(seed), 8)
    elem_stiff = draw_elem_stiff(jax.random.fold_in(seeds[7], 71), 0)
    density = jnp.clip(0.05 + 0.95 * jax.random.uniform(seeds[1], (ELEMS,), jnp.float32) ** level_of(seeds[1], (ELEMS,), ((0, 512),), -0.2, 0.2), 0.05, 1.0)
    owner_keys = jax.random.split(jax.random.fold_in(seeds[2], 1), PARENTS // PAR_DEV)
    owner_turns = jax.random.permutation(jax.random.fold_in(seeds[2], 3), PARENTS // PAR_DEV)
    owner = jax.vmap(lambda own, number: routed_block(jax.random.fold_in(seeds[2], 2), own, number, PAR_DEV, N_DEV, 1, CAP, 2))(owner_keys, owner_turns).reshape((PARENTS, 1))
    agg_slot = place_ends(jax.random.randint(seeds[3], (PARENTS,), 0, AGG_DEV), jax.random.fold_in(seeds[3], 1), 0, AGG_DEV - 1).astype(jnp.int32)
    par_octant = place_ends(jax.random.randint(seeds[4], (PARENTS,), 0, 8), jax.random.fold_in(seeds[4], 1), 0, 7).astype(jnp.int32)
    agg_octant = place_ends(jax.random.randint(seeds[5], (AGGS,), 0, 8), jax.random.fold_in(seeds[5], 1), 0, 7).astype(jnp.int32)
    coarse_map = place_ends(jax.random.randint(seeds[6], (AGGS,), 0, COARSE_DEV), jax.random.fold_in(seeds[6], 1), 0, COARSE_DEV - 1).astype(jnp.int32)
    return {"elem_stiff": elem_stiff, "density": density, "owner": owner, "agg_slot": agg_slot, "par_octant": par_octant, "agg_octant": agg_octant, "coarse_map": coarse_map}


def prolong_table():
    table = np.zeros((8, 24, 24), np.float32)
    for octant in range(8):
        for child in range(8):
            for corner in range(8):
                value = 1.0
                for bit in range(3):
                    place = (((octant >> bit) & 1) + ((child >> bit) & 1)) / 2.0
                    value = value * (place if (corner >> bit) & 1 else 1.0 - place)
                for comp in range(3):
                    table[octant, child * 3 + comp, corner * 3 + comp] = value
    return jnp.asarray(table)


def lift_cols(stiff, octants, table):
    count = stiff.shape[1]
    picks = (octants[None, :] == jnp.arange(8, dtype=jnp.int32)[:, None]).astype(jnp.float32)
    select = jnp.einsum('oia,on->ian', table, picks, precision=lax.Precision.HIGHEST)
    mats = stiff.reshape(24, 24, count)
    left = jnp.einsum('ijn,jbn->ibn', mats, select, precision=lax.Precision.HIGHEST)
    return jnp.einsum('ian,ibn->abn', select, left, precision=lax.Precision.HIGHEST).reshape(576, count)


def reference(elem_stiff, density, owner, agg_slot, par_octant, agg_octant, coarse_map):
    table = prolong_table()
    ranks = N_GRP * N_DEV
    elem_dev = ELEM_DEV
    par_dev = elem_dev // 8

    def one_device(index):
        start = index.astype(jnp.int32) * elem_dev
        block = lax.dynamic_slice_in_dim(elem_stiff, start, elem_dev, 1).astype(jnp.float32)
        dens = lax.dynamic_slice_in_dim(density, start, elem_dev, 0)
        weight = 0.001 + 0.999 * dens * dens * dens
        mats = block.reshape(24, 24, par_dev, 8)
        right = jnp.einsum('ijqo,ojb->ibqo', mats, table, precision=lax.Precision.HIGHEST)
        right = right * weight.reshape(par_dev, 8)[None, None]
        parent_mat = jnp.einsum('oia,ibqo->abq', table, right, precision=lax.Precision.HIGHEST)
        octs = lax.dynamic_slice_in_dim(par_octant, index.astype(jnp.int32) * par_dev, par_dev, 0)
        return lift_cols(parent_mat.reshape(576, par_dev), octs, table)

    sent = lax.map(one_device, jnp.arange(ranks, dtype=jnp.int32))
    rows = jnp.transpose(sent, (0, 2, 1)).reshape(ranks * par_dev, 576)
    slab = jnp.arange(ranks * par_dev, dtype=jnp.int32) // (N_DEV * par_dev)
    ids = (slab * N_DEV + owner[:, 0]) * AGG_DEV + agg_slot
    level_two = jax.ops.segment_sum(rows, ids, num_segments=ranks * AGG_DEV).T
    lifted = lift_cols(level_two, agg_octant, table)
    devs = (jnp.arange(ranks * AGG_DEV, dtype=jnp.int32) // AGG_DEV) % N_DEV
    coarse = jax.ops.segment_sum(lifted.T, devs * COARSE_DEV + coarse_map, num_segments=N_DEV * COARSE_DEV).T
    return level_two, coarse
```

```python
import functools

import jax
import jax.numpy as jnp
import ml_dtypes
import numpy as np
from jax import lax
from jax.experimental import pallas as pl
from jax.experimental.pallas import tpu as pltpu
from jax.sharding import PartitionSpec as P

MESH = pl.DeviceIdType.MESH
F32, BF16 = jnp.float32, jnp.bfloat16
MODES = 300
CODE = 300
COLS = 304
WIDE = 384
KEEP = ((0, 384), (400, 432), (448, 480), (496, 528), (544, 576))
SLOTS = 16
PACK = 40


def prolong_np():
    table = np.zeros((8, 24, 24))
    for octant in range(8):
        for child in range(8):
            for corner in range(8):
                value = 1.0
                for bit in range(3):
                    place = (((octant >> bit) & 1) + ((child >> bit) & 1)) / 2.0
                    value *= place if (corner >> bit) & 1 else 1.0 - place
                for comp in range(3):
                    table[octant, child * 3 + comp, corner * 3 + comp] = value
    return table


def constants():
    table = prolong_np()
    axis = np.array([[1.0, -1.0], [1.0, 1.0]])
    basis = np.kron(np.kron(np.kron(axis, axis), axis), np.eye(3))
    pairs = [(k, l) for k in range(24) for l in range(k, 24)]
    ks, ls = np.array([p[0] for p in pairs]), np.array([p[1] for p in pairs])
    kept = np.concatenate([np.arange(a, b) for a, b in KEEP])
    row_i, row_j = kept // 24, kept % 24
    used = row_i <= row_j
    off = (row_i != row_j)[None, :]
    first = np.zeros((8, COLS, kept.size))
    for octant in range(8):
        modes = table[octant] @ basis
        term = modes[row_i][:, ks].T * modes[row_j][:, ls].T
        swap = modes[row_j][:, ks].T * modes[row_i][:, ls].T
        first[octant, :MODES] = np.where(used[None, :], term + off * swap, 0.0)
    step = np.linalg.inv(basis) @ table[7] @ basis
    lift = np.zeros((WIDE, WIDE))
    lift[:MODES, :MODES] = step[ks][:, ks].T * step[ls][:, ls].T + (ks != ls)[None, :] * (step[ls][:, ks].T * step[ks][:, ls].T)
    signs = np.zeros((WIDE, 8))
    parity = (ks // 3) ^ (ls // 3)
    for octant in range(8):
        sign = np.ones(MODES)
        for bit in range(3):
            sign *= np.where((parity >> bit) & 1, 1.0 if (octant >> bit) & 1 else -1.0, 1.0)
        signs[:MODES, octant] = sign
    nodal = np.zeros((576, WIDE))
    a, b = np.arange(576) // 24, np.arange(576) % 24
    nodal[:, :MODES] = (basis[a][:, ks] * basis[b][:, ls] + (ks != ls)[None, :] * basis[a][:, ls] * basis[b][:, ks]) / 64.0
    cast = lambda array: np.asarray(array).astype(ml_dtypes.bfloat16)
    return cast(first), cast(lift), cast(signs), cast(nodal)


def mm(left, right, left_dim=1, right_dim=0):
    return lax.dot_general(left, right, (((left_dim,), (right_dim,)), ((), ())), preferred_element_type=F32)


def iota(shape, dim):
    return lax.broadcasted_iota(jnp.int32, shape, dim)


def halves(value):
    high = value.astype(BF16)
    return high, (value - high.astype(F32)).astype(BF16)


def ones_where(mask):
    return jnp.where(mask, 1.0, 0.0).astype(BF16)


def kernel(
    n_grp, n_dev,
    stiff, dens, owner, slot, par_oct, agg_oct, agg_map, first, lift, signs, nodal,
    level_out, coarse_out,
    stiff_v, dens_v, owner_v, slot_v, par_oct_v, agg_oct_v, agg_map_v, first_v, lift_v, signs_v, nodal_v,
    xt, outgo, income, parts, gathered, totals,
    in_sem, first_sem, stiff_sem, send_sem, recv_sem, part_send, part_recv, total_send, total_recv,
):
    me_g, me_d = lax.axis_index("grp"), lax.axis_index("dev")
    blocks = 8

    loads = []
    for index, (src, dst) in enumerate((
        (dens, dens_v), (owner, owner_v), (slot, slot_v), (par_oct, par_oct_v), (agg_oct, agg_oct_v),
        (agg_map, agg_map_v), (lift, lift_v), (signs, signs_v), (nodal, nodal_v),
    )):
        loads.append(pltpu.make_async_copy(src, dst, in_sem.at[index]))
    stiff_loads = [
        pltpu.make_async_copy(stiff.at[:, pl.ds(512 * c, 512)], stiff_v.at[:, pl.ds(512 * c, 512)], stiff_sem.at[c])
        for c in range(4)
    ]
    first_loads = [pltpu.make_async_copy(first.at[o], first_v.at[o], first_sem.at[o]) for o in range(8)]
    for load in loads[:6] + stiff_loads + loads[6:8] + first_loads + loads[8:]:
        load.start()

    barrier = pltpu.get_barrier_semaphore()

    def greet_dev(k, _):
        pl.semaphore_signal(barrier, inc=1, device_id={"dev": lax.rem(me_d + k, n_dev)}, device_id_type=MESH)
        return 0

    def greet_grp(k, _):
        pl.semaphore_signal(barrier, inc=1, device_id={"grp": lax.rem(me_g + k, n_grp)}, device_id_type=MESH)
        return 0

    lax.fori_loop(1, n_dev, greet_dev, 0)
    lax.fori_loop(1, n_grp, greet_grp, 0)

    for load in loads[:6]:
        load.wait()

    owner_row = owner_v[...]
    hits = iota((n_dev, 256), 0) == owner_row
    before = ones_where(iota((256, 256), 0) < iota((256, 256), 1))
    hits_f = jnp.where(hits, 1.0, 0.0)
    rank = jnp.sum(mm(hits_f.astype(BF16), before) * hits_f, axis=0, keepdims=True)
    place = owner_row * SLOTS + rank.astype(jnp.int32)
    code = slot_v[...].astype(F32) + 1.0

    pos = iota((256, 256), 0)
    perm = ones_where(iota((256, 256), 1) == 8 * (pos % 32) + pos // 32)

    dens_row = dens_v[...]
    dens_8 = jnp.concatenate([dens_row[:, 256 * b:256 * (b + 1)] for b in range(blocks)], axis=0)
    weight = 0.001 + 0.999 * dens_8 * dens_8 * dens_8
    one = weight.astype(BF16)
    rest = weight - one.astype(F32)
    two = rest.astype(BF16)
    three = (rest - two.astype(F32)).astype(BF16)
    pieces = jnp.concatenate([one.astype(F32), two.astype(F32), three.astype(F32)], axis=0).astype(BF16)
    turned = mm(perm, pieces, 1, 1).astype(BF16)
    spread = ones_where(iota((24, 256), 0) % 8 == iota((24, 256), 1) // 32)
    spread_w = mm(turned, spread)
    own_row = iota((256, 256), 0) % 32 == iota((256, 256), 1) % 32
    weights = jnp.sum(jnp.where(own_row, spread_w, 0.0).reshape(8, 32, 256), axis=1)

    for c in range(4):
        stiff_loads[c].wait()
        for b in (2 * c, 2 * c + 1):
            lanes = slice(256 * b, 256 * (b + 1))
            block = jnp.concatenate([stiff_v[a:z, lanes] for a, z in KEEP], axis=0)
            rows = mm(perm, block, 1, 1).astype(BF16)
            for o in range(8):
                xt[o, 32 * b:32 * (b + 1), :] = rows[32 * o:32 * (o + 1)]

    parent = None
    for o in range(8):
        first_loads[o].wait()
        term = mm(first_v[o], xt[o], 1, 1) * weights[o:o + 1, :]
        parent = term if parent is None else parent + term

    for load in loads[6:8]:
        load.wait()
    octs = ones_where(iota((8, 256), 0) == par_oct_v[...])
    flips = mm(signs_v[0:COLS, :], octs)
    high, low = halves(parent * flips)
    lift_c = lift_v[0:COLS, 0:COLS]
    sent = (mm(lift_c, high) + mm(lift_c, low)) * flips
    sent = jnp.where(iota((COLS, 256), 0) == CODE, code, sent)
    tail = sent[256:COLS]
    gap = jnp.zeros((16, 256), F32)
    full = jnp.concatenate([sent, gap, tail, gap], axis=0)
    high, low = halves(full)

    picks = ones_where(iota((n_dev * SLOTS, 256), 0) == place)
    chosen = mm(picks, high, 1, 1) + mm(picks, low, 1, 1)
    outgo[:, 0:16, :] = chosen[:, 0:128].reshape(n_dev, 16, 128)
    outgo[:, 16:32, :] = chosen[:, 128:256].reshape(n_dev, 16, 128)
    ends = chosen[:, 256:384].reshape(n_dev, 2, 8, 128)
    outgo[:, 32:40, :] = jnp.where(iota((n_dev, 8, 128), 2) < 64, ends[:, 0], ends[:, 1])

    pl.semaphore_wait(barrier, n_dev + n_grp - 2)

    def to_owner(k):
        peer = lax.rem(me_d + k, n_dev)
        return pltpu.make_async_remote_copy(
            src_ref=outgo.at[peer], dst_ref=income.at[me_d], send_sem=send_sem.at[peer],
            recv_sem=recv_sem.at[me_d], device_id={"dev": peer}, device_id_type=MESH,
        )

    def from_source(k):
        peer = lax.rem(me_d + k, n_dev)
        return pltpu.make_async_remote_copy(
            src_ref=outgo.at[peer], dst_ref=income.at[peer], send_sem=send_sem.at[peer],
            recv_sem=recv_sem.at[peer], device_id={"dev": peer}, device_id_type=MESH,
        )

    def start_owner(k, _):
        to_owner(k).start()
        return 0

    def end_source(k, _):
        from_source(k).wait_recv()
        return 0

    def end_owner(k, _):
        to_owner(k).wait_send()
        return 0

    lax.fori_loop(1, n_dev, start_owner, 0)
    income[me_d] = outgo[me_d]

    octs = ones_where(iota((8, 64), 0) == agg_oct_v[...])
    agg_flips = mm(octs, signs_v[...], 0, 1)
    sums = ones_where(iota((16, 64), 0) == agg_map_v[...])
    loads[8].wait()

    lax.fori_loop(1, n_dev, end_source, 0)

    lane = iota((8, 128), 1)
    code_at = ones_where(lane == CODE - 256 + 64 * iota((8, 128), 0))
    packed = income[:, 32:40, :].reshape(n_dev * 8, 128)
    codes = mm(code_at, packed.astype(BF16), 1, 1).astype(jnp.int32)
    level = []
    for h in range(2):
        into = ones_where(iota((64, n_dev * 8), 0) == codes[h:h + 1, :] - 1)
        wide = jnp.concatenate([
            income[:, 8 * h:8 * h + 8, :].reshape(n_dev * 8, 128),
            income[:, 16 + 8 * h:24 + 8 * h, :].reshape(n_dev * 8, 128),
            packed,
        ], axis=1)
        high, low = halves(wide)
        level.append(mm(into, high) + mm(into, low))
    ends = level[0][:, 256:] + pltpu.roll(level[1][:, 256:], 64, 1)
    ends = jnp.where(iota((64, 128), 1) < MODES - 256, ends, 0.0)
    level = jnp.concatenate([level[0][:, :256] + level[1][:, :256], ends], axis=1)

    both = jnp.concatenate(halves(level * agg_flips), axis=0)
    lifted = mm(both, lift_v[...], 1, 1)
    high, low = halves((lifted[0:64] + lifted[64:128]) * agg_flips)
    share = mm(sums, high) + mm(sums, low)
    for k in range(3):
        parts[:, k, :] = share[:, 128 * k:128 * (k + 1)]

    def to_adder(k):
        peer = lax.rem(me_g + k, n_grp)
        return pltpu.make_async_remote_copy(
            src_ref=parts.at[peer], dst_ref=gathered.at[me_g], send_sem=part_send.at[peer],
            recv_sem=part_recv.at[me_g], device_id={"grp": peer}, device_id_type=MESH,
        )

    def from_slab(k):
        peer = lax.rem(me_g + k, n_grp)
        return pltpu.make_async_remote_copy(
            src_ref=parts.at[peer], dst_ref=gathered.at[peer], send_sem=part_send.at[peer],
            recv_sem=part_recv.at[peer], device_id={"grp": peer}, device_id_type=MESH,
        )

    def to_all(k):
        peer = lax.rem(me_g + k, n_grp)
        return pltpu.make_async_remote_copy(
            src_ref=totals.at[me_g], dst_ref=totals.at[me_g], send_sem=total_send.at[peer],
            recv_sem=total_recv.at[me_g], device_id={"grp": peer}, device_id_type=MESH,
        )

    def from_adder(k):
        peer = lax.rem(me_g + k, n_grp)
        return pltpu.make_async_remote_copy(
            src_ref=totals.at[me_g], dst_ref=totals.at[peer], send_sem=total_send.at[peer],
            recv_sem=total_recv.at[peer], device_id={"grp": peer}, device_id_type=MESH,
        )

    def loop(make, act):
        def run(k, _):
            getattr(make(k), act)()
            return 0
        lax.fori_loop(1, n_grp, run, 0)

    loop(to_adder, "start")
    gathered[me_g] = parts[me_g]

    high, low = halves(level)
    level_out[...] = mm(high, nodal_v[...], 1, 1) + mm(low, nodal_v[...], 1, 1)

    loop(from_slab, "wait_recv")
    totals[me_g] = jnp.sum(gathered[...], axis=0)
    loop(to_all, "start")
    lax.fori_loop(1, n_dev, end_owner, 0)
    loop(to_adder, "wait_send")
    loop(from_adder, "wait_recv")

    coarse = jnp.concatenate([totals[:, k, :] for k in range(3)], axis=1)
    high, low = halves(coarse)
    coarse_out[...] = mm(high, nodal_v[...], 1, 1) + mm(low, nodal_v[...], 1, 1)
    loop(to_all, "wait_send")


def body(n_grp, n_dev, elem_stiff, density, owner, agg_slot, par_octant, agg_octant, coarse_map):
    first, lift, signs, nodal = constants()
    row = lambda array: array.reshape(1, -1)
    args = (
        elem_stiff, row(density), row(owner), row(agg_slot), row(par_octant), row(agg_octant), row(coarse_map),
        jnp.asarray(first), jnp.asarray(lift), jnp.asarray(signs), jnp.asarray(nodal),
    )
    dma = pltpu.SemaphoreType.DMA
    level, coarse = pl.pallas_call(
        functools.partial(kernel, n_grp, n_dev),
        out_shape=(jax.ShapeDtypeStruct((64, 576), F32), jax.ShapeDtypeStruct((16, 576), F32)),
        in_specs=[pl.BlockSpec(memory_space=pl.ANY)] * len(args),
        out_specs=(pl.BlockSpec(memory_space=pltpu.VMEM), pl.BlockSpec(memory_space=pltpu.VMEM)),
        scratch_shapes=[pltpu.VMEM(a.shape, a.dtype) for a in args] + [
            pltpu.VMEM((8, 256, 512), BF16),
            pltpu.VMEM((n_dev, PACK, 128), F32),
            pltpu.VMEM((n_dev, PACK, 128), F32),
            pltpu.VMEM((n_grp, 3, 128), F32),
            pltpu.VMEM((n_grp, 3, 128), F32),
            pltpu.VMEM((n_grp, 3, 128), F32),
            dma((9,)), dma((8,)), dma((4,)), dma((n_dev,)), dma((n_dev,)),
            dma((n_grp,)), dma((n_grp,)), dma((n_grp,)), dma((n_grp,)),
        ],
        compiler_params=pltpu.CompilerParams(
            collective_id=0, has_side_effects=True, vmem_limit_bytes=48 * 1024 * 1024
        ),
    )(*args)
    return level.T, coarse.T


def solution(mesh):
    split = P(("grp", "dev"))
    return jax.shard_map(
        functools.partial(body, mesh.shape["grp"], mesh.shape["dev"]),
        mesh=mesh,
        in_specs=(P(None, ("grp", "dev")), split, P(("grp", "dev"), None), split, split, split, split),
        out_specs=(P(None, ("grp", "dev")), P(None, "dev")),
        check_vma=False,
    )
```

```python
import functools

import jax
import jax.numpy as jnp
import ml_dtypes
import numpy as np
from jax import lax
from jax.experimental import pallas as pl
from jax.experimental.pallas import tpu as pltpu
from jax.sharding import PartitionSpec as P

MESH = pl.DeviceIdType.MESH
F32, BF16 = jnp.float32, jnp.bfloat16
MODES = 300
CODE = 300
COLS = 304
WIDE = 384
KEEP = ((0, 384), (400, 432), (448, 480), (496, 528), (544, 576))
SLOTS = 16
FAR_FIRST = sorted(
    [(dx, dy, dc) for dx in range(4) for dy in range(4) for dc in range(2) if dx + dy + dc],
    key=lambda step: -(min(step[0], 4 - step[0]) + min(step[1], 4 - step[1])),
)
TEAM = 4
PACK = 40


def prolong_np():
    table = np.zeros((8, 24, 24))
    for octant in range(8):
        for child in range(8):
            for corner in range(8):
                value = 1.0
                for bit in range(3):
                    place = (((octant >> bit) & 1) + ((child >> bit) & 1)) / 2.0
                    value *= place if (corner >> bit) & 1 else 1.0 - place
                for comp in range(3):
                    table[octant, child * 3 + comp, corner * 3 + comp] = value
    return table


def constants():
    table = prolong_np()
    axis = np.array([[1.0, -1.0], [1.0, 1.0]])
    basis = np.kron(np.kron(np.kron(axis, axis), axis), np.eye(3))
    pairs = [(k, l) for k in range(24) for l in range(k, 24)]
    ks, ls = np.array([p[0] for p in pairs]), np.array([p[1] for p in pairs])
    kept = np.concatenate([np.arange(a, b) for a, b in KEEP])
    row_i, row_j = kept // 24, kept % 24
    used = row_i <= row_j
    off = (row_i != row_j)[None, :]
    first = np.zeros((8, COLS, kept.size))
    for octant in range(8):
        modes = table[octant] @ basis
        term = modes[row_i][:, ks].T * modes[row_j][:, ls].T
        swap = modes[row_j][:, ks].T * modes[row_i][:, ls].T
        first[octant, :MODES] = np.where(used[None, :], term + off * swap, 0.0)
    step = np.linalg.inv(basis) @ table[7] @ basis
    lift = np.zeros((WIDE, WIDE))
    lift[:MODES, :MODES] = step[ks][:, ks].T * step[ls][:, ls].T + (ks != ls)[None, :] * (step[ls][:, ks].T * step[ks][:, ls].T)
    signs = np.zeros((WIDE, 8))
    parity = (ks // 3) ^ (ls // 3)
    for octant in range(8):
        sign = np.ones(MODES)
        for bit in range(3):
            sign *= np.where((parity >> bit) & 1, 1.0 if (octant >> bit) & 1 else -1.0, 1.0)
        signs[:MODES, octant] = sign
    nodal = np.zeros((576, WIDE))
    a, b = np.arange(576) // 24, np.arange(576) % 24
    nodal[:, :MODES] = (basis[a][:, ks] * basis[b][:, ls] + (ks != ls)[None, :] * basis[a][:, ls] * basis[b][:, ks]) / 64.0
    cast = lambda array: np.asarray(array).astype(ml_dtypes.bfloat16)
    return cast(first), cast(lift), cast(signs), cast(nodal)


def mm(left, right, left_dim=1, right_dim=0):
    return lax.dot_general(left, right, (((left_dim,), (right_dim,)), ((), ())), preferred_element_type=F32)


def iota(shape, dim):
    return lax.broadcasted_iota(jnp.int32, shape, dim)


def halves(value):
    high = value.astype(BF16)
    return high, (value - high.astype(F32)).astype(BF16)


def ones_where(mask):
    return jnp.where(mask, 1.0, 0.0).astype(BF16)


def kernel(
    n_grp, n_dev,
    stiff, dens, owner, slot, par_oct, agg_oct, agg_map, first, lift, signs, nodal,
    level_out, coarse_out,
    stiff_v, dens_v, owner_v, slot_v, par_oct_v, agg_oct_v, agg_map_v, first_v, lift_v, signs_v, nodal_v,
    xt, outgo, income, parts, gathered, totals,
    in_sem, first_sem, stiff_sem, send_sem, recv_sem, part_send, part_recv, total_send, total_recv,
):
    me_g, me_d = lax.axis_index("grp"), lax.axis_index("dev")
    blocks = 8

    loads = []
    for index, (src, dst) in enumerate((
        (dens, dens_v), (owner, owner_v), (slot, slot_v), (par_oct, par_oct_v), (agg_oct, agg_oct_v),
        (agg_map, agg_map_v), (lift, lift_v), (signs, signs_v), (nodal, nodal_v),
    )):
        loads.append(pltpu.make_async_copy(src, dst, in_sem.at[index]))
    stiff_loads = [
        pltpu.make_async_copy(stiff.at[:, pl.ds(1024 * c, 1024)], stiff_v.at[:, pl.ds(1024 * c, 1024)], stiff_sem.at[c])
        for c in range(2)
    ]
    first_loads = [pltpu.make_async_copy(first, first_v, first_sem.at[0])]
    for load in loads[:6] + stiff_loads + loads[6:8] + first_loads + loads[8:]:
        load.start()

    barrier = pltpu.get_barrier_semaphore()

    def greet_dev(k, _):
        pl.semaphore_signal(barrier, inc=1, device_id={"dev": lax.rem(me_d + k, n_dev)}, device_id_type=MESH)
        return 0

    def greet_grp(k, _):
        pl.semaphore_signal(barrier, inc=1, device_id={"grp": lax.rem(me_g + k, n_grp)}, device_id_type=MESH)
        return 0

    lax.fori_loop(1, n_dev, greet_dev, 0)
    lax.fori_loop(1, n_grp, greet_grp, 0)

    for load in loads[:6]:
        load.wait()

    owner_row = owner_v[...]
    hits = iota((n_dev, 256), 0) == owner_row
    before = ones_where(iota((256, 256), 0) < iota((256, 256), 1))
    hits_f = jnp.where(hits, 1.0, 0.0)
    rank = jnp.sum(mm(hits_f.astype(BF16), before) * hits_f, axis=0, keepdims=True)
    place = owner_row * SLOTS + rank.astype(jnp.int32)
    code = slot_v[...].astype(F32) + 1.0

    pos = iota((256, 256), 0)
    perm = ones_where(iota((256, 256), 1) == 8 * (pos % 32) + pos // 32)

    dens_row = dens_v[...]
    dens_8 = jnp.concatenate([dens_row[:, 256 * b:256 * (b + 1)] for b in range(blocks)], axis=0)
    weight = 0.001 + 0.999 * dens_8 * dens_8 * dens_8
    one = weight.astype(BF16)
    rest = weight - one.astype(F32)
    two = rest.astype(BF16)
    three = (rest - two.astype(F32)).astype(BF16)
    pieces = jnp.concatenate([one.astype(F32), two.astype(F32), three.astype(F32)], axis=0).astype(BF16)
    turned = mm(perm, pieces, 1, 1).astype(BF16)
    spread = ones_where(iota((24, 256), 0) % 8 == iota((24, 256), 1) // 32)
    spread_w = mm(turned, spread)
    own_row = iota((256, 256), 0) % 32 == iota((256, 256), 1) % 32
    weights = jnp.sum(jnp.where(own_row, spread_w, 0.0).reshape(8, 32, 256), axis=1)

    for c in range(2):
        stiff_loads[c].wait()
        for b in range(4 * c, 4 * c + 4):
            lanes = slice(256 * b, 256 * (b + 1))
            block = jnp.concatenate([stiff_v[a:z, lanes] for a, z in KEEP], axis=0)
            rows = mm(perm, block, 1, 1).astype(BF16)
            for o in range(8):
                xt[o, 32 * b:32 * (b + 1), :] = rows[32 * o:32 * (o + 1)]

    parent = None
    first_loads[0].wait()
    for load in loads[6:8]:
        load.wait()
    for o in range(8):
        term = mm(first_v[o], xt[o], 1, 1) * weights[o:o + 1, :]
        parent = term if parent is None else parent + term

    octs = ones_where(iota((8, 256), 0) == par_oct_v[...])
    flips = mm(signs_v[0:COLS, :], octs)
    high, low = halves(parent * flips)
    lift_c = lift_v[0:COLS, 0:COLS]
    sent = (mm(lift_c, high) + mm(lift_c, low)) * flips
    sent = jnp.where(iota((COLS, 256), 0) == CODE, code, sent)
    tail = sent[256:COLS]
    gap = jnp.zeros((16, 256), F32)
    full = jnp.concatenate([sent, gap, tail, gap], axis=0)
    high, low = halves(full)

    picks = ones_where(iota((n_dev * SLOTS, 256), 0) == place)
    chosen = mm(picks, high, 1, 1) + mm(picks, low, 1, 1)
    outgo[:, 0:16, :] = chosen[:, 0:128].reshape(n_dev, 16, 128)
    outgo[:, 16:32, :] = chosen[:, 128:256].reshape(n_dev, 16, 128)
    ends = chosen[:, 256:384].reshape(n_dev, 2, 8, 128)
    outgo[:, 32:40, :] = jnp.where(iota((n_dev, 8, 128), 2) < 64, ends[:, 0], ends[:, 1])

    pl.semaphore_wait(barrier, n_dev + n_grp - 2)

    def to_owner(peer):
        return pltpu.make_async_remote_copy(
            src_ref=outgo.at[peer], dst_ref=income.at[me_d], send_sem=send_sem.at[peer],
            recv_sem=recv_sem.at[me_d], device_id={"dev": peer}, device_id_type=MESH,
        )

    def from_source(peer):
        return pltpu.make_async_remote_copy(
            src_ref=outgo.at[peer], dst_ref=income.at[peer], send_sem=send_sem.at[peer],
            recv_sem=recv_sem.at[peer], device_id={"dev": peer}, device_id_type=MESH,
        )

    def end_source(k, _):
        from_source(lax.rem(me_d + k, n_dev)).wait_recv()
        return 0

    def end_owner(k, _):
        to_owner(lax.rem(me_d + k, n_dev)).wait_send()
        return 0

    x, y, core = lax.div(me_d, 8), lax.rem(lax.div(me_d, 2), 4), lax.rem(me_d, 2)
    for dx, dy, dc in FAR_FIRST:
        to_owner((lax.rem(x + dx, 4) * 4 + lax.rem(y + dy, 4)) * 2 + lax.rem(core + dc, 2)).start()
    income[me_d] = outgo[me_d]

    octs = ones_where(iota((8, 64), 0) == agg_oct_v[...])
    agg_flips = mm(octs, signs_v[...], 0, 1)
    sums = ones_where(iota((16, 64), 0) == agg_map_v[...])
    loads[8].wait()

    lax.fori_loop(1, n_dev, end_source, 0)

    lane = iota((8, 128), 1)
    code_at = ones_where(lane == CODE - 256 + 64 * iota((8, 128), 0))
    packed = income[:, 32:40, :].reshape(n_dev * 8, 128)
    codes = mm(code_at, packed.astype(BF16), 1, 1).astype(jnp.int32)
    level = []
    for h in range(2):
        into = ones_where(iota((64, n_dev * 8), 0) == codes[h:h + 1, :] - 1)
        wide = jnp.concatenate([
            income[:, 8 * h:8 * h + 8, :].reshape(n_dev * 8, 128),
            income[:, 16 + 8 * h:24 + 8 * h, :].reshape(n_dev * 8, 128),
            packed,
        ], axis=1)
        high, low = halves(wide)
        level.append(mm(into, high) + mm(into, low))
    ends = level[0][:, 256:] + pltpu.roll(level[1][:, 256:], 64, 1)
    ends = jnp.where(iota((64, 128), 1) < MODES - 256, ends, 0.0)
    level = jnp.concatenate([level[0][:, :256] + level[1][:, :256], ends], axis=1)

    both = jnp.concatenate(halves(level * agg_flips), axis=0)
    lifted = mm(both, lift_v[...], 1, 1)
    high, low = halves((lifted[0:64] + lifted[64:128]) * agg_flips)
    share = mm(sums, high) + mm(sums, low)
    for t in range(TEAM):
        for k in range(3):
            parts[t, 4 * k:4 * k + 4, :] = share[4 * t:4 * t + 4, 128 * k:128 * (k + 1)]

    mine = lax.rem(me_g, TEAM)
    base = me_g - mine

    def in_team(k, sending):
        other = lax.rem(mine + k, TEAM)
        return pltpu.make_async_remote_copy(
            src_ref=parts.at[other], dst_ref=gathered.at[mine if sending else other], send_sem=part_send.at[other],
            recv_sem=part_recv.at[mine if sending else other], device_id={"grp": base + other}, device_id_type=MESH,
        )

    def to_all(k, sending):
        peer = lax.rem(me_g + k, n_grp)
        return pltpu.make_async_remote_copy(
            src_ref=totals.at[me_g], dst_ref=totals.at[me_g if sending else peer], send_sem=total_send.at[peer],
            recv_sem=total_recv.at[me_g if sending else peer], device_id={"grp": peer}, device_id_type=MESH,
        )

    for k in (2, 1, 3):
        in_team(k, True).start()
    gathered[mine] = parts[mine]
    for k in (2, 1, 3):
        in_team(k, False).wait_recv()
    totals[me_g] = (gathered[0] + gathered[1]) + (gathered[2] + gathered[3])
    for k in (8, 7, 9, 6, 10, 5, 11, 4, 12, 3, 13, 2, 14, 1, 15):
        to_all(k, True).start()

    high, low = halves(level)
    level_out[...] = mm(high, nodal_v[...], 1, 1) + mm(low, nodal_v[...], 1, 1)
    lax.fori_loop(1, n_dev, end_owner, 0)
    for k in (1, 2, 3):
        in_team(k, True).wait_send()

    def end_all(k, _):
        to_all(k, False).wait_recv()
        return 0

    def end_sent(k, _):
        to_all(k, True).wait_send()
        return 0

    lax.fori_loop(1, n_grp, end_all, 0)
    coarse = []
    for k in range(3):
        quarters = []
        for t in range(TEAM):
            rows = [totals[TEAM * u + t, 4 * k:4 * k + 4, :] for u in range(n_grp // TEAM)]
            quarters.append((rows[0] + rows[1]) + (rows[2] + rows[3]))
        coarse.append(jnp.concatenate(quarters, axis=0))
    high, low = halves(jnp.concatenate(coarse, axis=1))
    coarse_out[...] = mm(high, nodal_v[...], 1, 1) + mm(low, nodal_v[...], 1, 1)
    lax.fori_loop(1, n_grp, end_sent, 0)


def body(n_grp, n_dev, elem_stiff, density, owner, agg_slot, par_octant, agg_octant, coarse_map):
    first, lift, signs, nodal = constants()
    row = lambda array: array.reshape(1, -1)
    args = (
        elem_stiff, row(density), row(owner), row(agg_slot), row(par_octant), row(agg_octant), row(coarse_map),
        jnp.asarray(first), jnp.asarray(lift), jnp.asarray(signs), jnp.asarray(nodal),
    )
    dma = pltpu.SemaphoreType.DMA
    level, coarse = pl.pallas_call(
        functools.partial(kernel, n_grp, n_dev),
        out_shape=(pltpu.VMEM((64, 576), F32), pltpu.VMEM((16, 576), F32)),
        in_specs=[pl.BlockSpec(memory_space=pltpu.HBM)] * len(args),
        out_specs=(pl.BlockSpec(memory_space=pltpu.VMEM), pl.BlockSpec(memory_space=pltpu.VMEM)),
        scratch_shapes=[pltpu.VMEM(a.shape, a.dtype) for a in args] + [
            pltpu.VMEM((8, 256, 512), BF16),
            pltpu.VMEM((n_dev, PACK, 128), F32),
            pltpu.VMEM((n_dev, PACK, 128), F32),
            pltpu.VMEM((TEAM, 12, 128), F32),
            pltpu.VMEM((TEAM, 12, 128), F32),
            pltpu.VMEM((n_grp, 12, 128), F32),
            dma((9,)), dma((1,)), dma((2,)), dma((n_dev,)), dma((n_dev,)),
            dma((TEAM,)), dma((TEAM,)), dma((n_grp,)), dma((n_grp,)),
        ],
        compiler_params=pltpu.CompilerParams(
            collective_id=0, has_side_effects=True, vmem_limit_bytes=63 * 1024 * 1024
        ),
    )(*args)
    return level.T, coarse.T


def solution(mesh):
    split = P(("grp", "dev"))
    return jax.shard_map(
        functools.partial(body, mesh.shape["grp"], mesh.shape["dev"]),
        mesh=mesh,
        in_specs=(P(None, ("grp", "dev")), split, P(("grp", "dev"), None), split, split, split, split),
        out_specs=(P(None, ("grp", "dev")), P(None, "dev")),
        check_vma=False,
    )
```

```python
import functools

import jax
import jax.numpy as jnp
import ml_dtypes
import numpy as np
from jax import lax
from jax.experimental import pallas as pl
from jax.experimental.pallas import tpu as pltpu
from jax.sharding import PartitionSpec as P

MESH = pl.DeviceIdType.MESH
F32, BF16 = jnp.float32, jnp.bfloat16
MODES = 300
CODE = 300
COLS = 304
WIDE = 384
KEEP = ((0, 384), (400, 432), (448, 480), (496, 528), (544, 576))
SLOTS = 16
FAR_FIRST = sorted(
    [(dx, dy, dc) for dx in range(4) for dy in range(4) for dc in range(2) if dx + dy + dc],
    key=lambda step: -(min(step[0], 4 - step[0]) + min(step[1], 4 - step[1])),
)
HANDED = (8, 9, 10, 11, 12, 13, 14)
PACK = 40


def prolong_np():
    table = np.zeros((8, 24, 24))
    for octant in range(8):
        for child in range(8):
            for corner in range(8):
                value = 1.0
                for bit in range(3):
                    place = (((octant >> bit) & 1) + ((child >> bit) & 1)) / 2.0
                    value *= place if (corner >> bit) & 1 else 1.0 - place
                for comp in range(3):
                    table[octant, child * 3 + comp, corner * 3 + comp] = value
    return table


def constants():
    table = prolong_np()
    axis = np.array([[1.0, -1.0], [1.0, 1.0]])
    basis = np.kron(np.kron(np.kron(axis, axis), axis), np.eye(3))
    pairs = [(k, l) for k in range(24) for l in range(k, 24)]
    ks, ls = np.array([p[0] for p in pairs]), np.array([p[1] for p in pairs])
    kept = np.concatenate([np.arange(a, b) for a, b in KEEP])
    row_i, row_j = kept // 24, kept % 24
    used = row_i <= row_j
    off = (row_i != row_j)[None, :]
    first = np.zeros((8, COLS, kept.size))
    for octant in range(8):
        modes = table[octant] @ basis
        term = modes[row_i][:, ks].T * modes[row_j][:, ls].T
        swap = modes[row_j][:, ks].T * modes[row_i][:, ls].T
        first[octant, :MODES] = np.where(used[None, :], term + off * swap, 0.0)
    step = np.linalg.inv(basis) @ table[7] @ basis
    lift = np.zeros((WIDE, WIDE))
    lift[:MODES, :MODES] = step[ks][:, ks].T * step[ls][:, ls].T + (ks != ls)[None, :] * (step[ls][:, ks].T * step[ks][:, ls].T)
    signs = np.zeros((WIDE, 8))
    parity = (ks // 3) ^ (ls // 3)
    for octant in range(8):
        sign = np.ones(MODES)
        for bit in range(3):
            sign *= np.where((parity >> bit) & 1, 1.0 if (octant >> bit) & 1 else -1.0, 1.0)
        signs[:MODES, octant] = sign
    nodal = np.zeros((576, WIDE))
    a, b = np.arange(576) // 24, np.arange(576) % 24
    nodal[:, :MODES] = (basis[a][:, ks] * basis[b][:, ls] + (ks != ls)[None, :] * basis[a][:, ls] * basis[b][:, ks]) / 64.0
    cast = lambda array: np.asarray(array).astype(ml_dtypes.bfloat16)
    return cast(first), cast(lift), cast(signs), cast(nodal)


def mm(left, right, left_dim=1, right_dim=0):
    return lax.dot_general(left, right, (((left_dim,), (right_dim,)), ((), ())), preferred_element_type=F32)


def iota(shape, dim):
    return lax.broadcasted_iota(jnp.int32, shape, dim)


def halves(value):
    high = value.astype(BF16)
    return high, (value - high.astype(F32)).astype(BF16)


def ones_where(mask):
    return jnp.where(mask, 1.0, 0.0).astype(BF16)


def kernel(
    n_grp, n_dev,
    stiff, dens, owner, slot, par_oct, agg_oct, agg_map, first, lift, signs, nodal,
    level_out, coarse_out,
    stiff_v, dens_v, owner_v, slot_v, par_oct_v, agg_oct_v, agg_map_v, first_v, lift_v, signs_v, nodal_v,
    xt, outgo, income, parts, gathered, totals,
    in_sem, first_sem, stiff_sem, send_sem, recv_sem, part_send, part_recv, total_send, total_recv,
):
    me_g, me_d = lax.axis_index("grp"), lax.axis_index("dev")
    blocks = 8

    small = [
        pltpu.make_async_copy(src, dst, in_sem.at[index])
        for index, (src, dst) in enumerate((
            (dens, dens_v), (owner, owner_v), (slot, slot_v), (par_oct, par_oct_v),
            (agg_oct, agg_oct_v), (agg_map, agg_map_v), (signs, signs_v),
        ))
    ]
    lift_load = pltpu.make_async_copy(lift, lift_v, in_sem.at[7])
    nodal_load = pltpu.make_async_copy(nodal, nodal_v, in_sem.at[8])
    first_load = pltpu.make_async_copy(first, first_v, first_sem.at[0])
    stiff_loads = [
        pltpu.make_async_copy(stiff.at[:, pl.ds(1024 * c, 1024)], stiff_v.at[:, pl.ds(1024 * c, 1024)], stiff_sem.at[c])
        for c in range(2)
    ]
    for load in stiff_loads + small + [first_load, lift_load, nodal_load]:
        load.start()

    barrier = pltpu.get_barrier_semaphore()

    def greet_dev(k, _):
        pl.semaphore_signal(barrier, inc=1, device_id={"dev": lax.rem(me_d + k, n_dev)}, device_id_type=MESH)
        return 0

    def greet_grp(k, _):
        pl.semaphore_signal(barrier, inc=1, device_id={"grp": k}, device_id_type=MESH)
        return 0

    lax.fori_loop(1, n_dev, greet_dev, 0)

    @pl.when(me_g == 0)
    def _():
        lax.fori_loop(1, n_grp, greet_grp, 0)

    @pl.when((me_g >= 8) & (me_g <= 14))
    def _():
        greet_grp(15, 0)

    @pl.when(((me_g >= 1) & (me_g <= 7)) | (me_g == 15))
    def _():
        greet_grp(0, 0)

    pos = iota((256, 256), 0)
    perm = ones_where(iota((256, 256), 1) == 8 * (pos % 32) + pos // 32)

    def turn(b):
        lanes = slice(256 * b, 256 * (b + 1))
        block = jnp.concatenate([stiff_v[a:z, lanes] for a, z in KEEP], axis=0)
        rows = mm(perm, block, 1, 1).astype(BF16)
        for o in range(8):
            xt[o, 32 * b:32 * (b + 1), :] = rows[32 * o:32 * (o + 1)]

    for load in stiff_loads + small:
        load.wait()
    for b in range(8):
        turn(b)

    owner_row = owner_v[...]
    hits = iota((n_dev, 256), 0) == owner_row
    before = ones_where(iota((256, 256), 0) < iota((256, 256), 1))
    hits_f = jnp.where(hits, 1.0, 0.0)
    rank = jnp.sum(mm(hits_f.astype(BF16), before) * hits_f, axis=0, keepdims=True)
    place = owner_row * SLOTS + rank.astype(jnp.int32)
    code = slot_v[...].astype(F32) + 1.0

    picks = ones_where(iota((n_dev * SLOTS, 256), 0) == place)

    dens_row = dens_v[...]
    dens_8 = jnp.concatenate([dens_row[:, 256 * b:256 * (b + 1)] for b in range(blocks)], axis=0)
    weight = 0.001 + 0.999 * dens_8 * dens_8 * dens_8
    one = weight.astype(BF16)
    rest = weight - one.astype(F32)
    two = rest.astype(BF16)
    three = (rest - two.astype(F32)).astype(BF16)
    pieces = jnp.concatenate([one.astype(F32), two.astype(F32), three.astype(F32)], axis=0).astype(BF16)
    turned = mm(perm, pieces, 1, 1).astype(BF16)
    spread = ones_where(iota((24, 256), 0) % 8 == iota((24, 256), 1) // 32)
    spread_w = mm(turned, spread)
    own_row = iota((256, 256), 0) % 32 == iota((256, 256), 1) % 32
    weights = jnp.sum(jnp.where(own_row, spread_w, 0.0).reshape(8, 32, 256), axis=1)

    octs = ones_where(iota((8, 256), 0) == par_oct_v[...])
    flips = mm(signs_v[0:COLS, :], octs)

    first_load.wait()
    lift_load.wait()
    parent = None
    for o in range(8):
        term = mm(first_v[o], xt[o], 1, 1) * weights[o:o + 1, :]
        parent = term if parent is None else parent + term

    high, low = halves(parent * flips)
    lift_c = lift_v[0:COLS, 0:COLS]
    sent = (mm(lift_c, high) + mm(lift_c, low)) * flips
    sent = jnp.where(iota((COLS, 256), 0) == CODE, code, sent)
    tail = sent[256:COLS]
    gap = jnp.zeros((16, 256), F32)
    full = jnp.concatenate([sent, gap, tail, gap], axis=0)
    high, low = halves(full)

    chosen = mm(picks, high, 1, 1) + mm(picks, low, 1, 1)
    outgo[:, 0:16, :] = chosen[:, 0:128].reshape(n_dev, 16, 128)
    outgo[:, 16:32, :] = chosen[:, 128:256].reshape(n_dev, 16, 128)
    ends = chosen[:, 256:384].reshape(n_dev, 2, 8, 128)
    outgo[:, 32:40, :] = jnp.where(iota((n_dev, 8, 128), 2) < 64, ends[:, 0], ends[:, 1])

    @pl.when((me_g == 0) | (me_g == 15))
    def _():
        pl.semaphore_wait(barrier, n_dev - 1 + 8)

    @pl.when((me_g >= 1) & (me_g <= 14))
    def _():
        pl.semaphore_wait(barrier, n_dev)

    def to_owner(peer):
        return pltpu.make_async_remote_copy(
            src_ref=outgo.at[peer], dst_ref=income.at[me_d], send_sem=send_sem.at[peer],
            recv_sem=recv_sem.at[me_d], device_id={"dev": peer}, device_id_type=MESH,
        )

    def from_source(peer):
        return pltpu.make_async_remote_copy(
            src_ref=outgo.at[peer], dst_ref=income.at[peer], send_sem=send_sem.at[peer],
            recv_sem=recv_sem.at[peer], device_id={"dev": peer}, device_id_type=MESH,
        )

    def end_source(k, _):
        from_source(lax.rem(me_d + k, n_dev)).wait_recv()
        return 0

    def end_owner(k, _):
        to_owner(lax.rem(me_d + k, n_dev)).wait_send()
        return 0

    x, y, core = lax.div(me_d, 8), lax.rem(lax.div(me_d, 2), 4), lax.rem(me_d, 2)
    for dx, dy, dc in FAR_FIRST:
        to_owner((lax.rem(x + dx, 4) * 4 + lax.rem(y + dy, 4)) * 2 + lax.rem(core + dc, 2)).start()
    income[me_d] = outgo[me_d]

    octs = ones_where(iota((8, 64), 0) == agg_oct_v[...])
    agg_flips = mm(octs, signs_v[...], 0, 1)
    sums = ones_where(iota((16, 64), 0) == agg_map_v[...])
    nodal_load.wait()

    lax.fori_loop(1, n_dev, end_source, 0)

    lane = iota((8, 128), 1)
    code_at = ones_where(lane == CODE - 256 + 64 * iota((8, 128), 0))
    packed = income[:, 32:40, :].reshape(n_dev * 8, 128)
    codes = mm(code_at, packed.astype(BF16), 1, 1).astype(jnp.int32)
    level = []
    for h in range(2):
        into = ones_where(iota((64, n_dev * 8), 0) == codes[h:h + 1, :] - 1)
        wide = jnp.concatenate([
            income[:, 8 * h:8 * h + 8, :].reshape(n_dev * 8, 128),
            income[:, 16 + 8 * h:24 + 8 * h, :].reshape(n_dev * 8, 128),
            packed,
        ], axis=1)
        high, low = halves(wide)
        level.append(mm(into, high) + mm(into, low))
    ends = level[0][:, 256:] + pltpu.roll(level[1][:, 256:], 64, 1)
    ends = jnp.where(iota((64, 128), 1) < MODES - 256, ends, 0.0)
    level = jnp.concatenate([level[0][:, :256] + level[1][:, :256], ends], axis=1)

    both = jnp.concatenate(halves(level * agg_flips), axis=0)
    lifted = mm(both, lift_v[...], 1, 1)
    high, low = halves((lifted[0:64] + lifted[64:128]) * agg_flips)
    share = mm(sums, high) + mm(sums, low)
    parts[0:16, :] = share[:, 0:128]
    parts[16:32, :] = share[:, 128:256]
    parts[32:40, :] = jnp.where(iota((8, 128), 1) < 64, share[0:8, 256:384], pltpu.roll(share[8:16, 256:384], 64, 1))

    def to_root(source):
        return pltpu.make_async_remote_copy(
            src_ref=parts, dst_ref=gathered.at[source], send_sem=part_send.at[0],
            recv_sem=part_recv.at[source], device_id={"grp": 0}, device_id_type=MESH,
        )

    def from_root(target):
        return pltpu.make_async_remote_copy(
            src_ref=totals, dst_ref=totals, send_sem=total_send.at[target],
            recv_sem=total_recv.at[0], device_id={"grp": target}, device_id_type=MESH,
        )

    @pl.when(me_g > 0)
    def _():
        to_root(me_g).start()

    high, low = halves(level)
    level_out[...] = mm(high, nodal_v[...], 1, 1) + mm(low, nodal_v[...], 1, 1)
    lax.fori_loop(1, n_dev, end_owner, 0)

    @pl.when(me_g == 0)
    def _():
        def end_part(k, _):
            to_root(k).wait_recv()
            return 0

        lax.fori_loop(1, n_grp, end_part, 0)
        sums = [parts[...]] + [gathered[k] for k in range(1, n_grp)]
        while len(sums) > 1:
            sums = [sums[k] + sums[k + 1] for k in range(0, len(sums), 2)]
        totals[...] = sums[0]
        for k in (1, 2, 15, 3, 4, 5, 6, 7):
            from_root(k).start()

    @pl.when(me_g > 0)
    def _():
        from_root(me_g).wait_recv()

    @pl.when(me_g == 15)
    def _():
        for k in HANDED:
            from_root(k).start()

    ends = totals[32:40, :]
    ends = jnp.concatenate([ends, pltpu.roll(ends, 64, 1)], axis=0)
    high, low = halves(jnp.concatenate([totals[0:16, :], totals[16:32, :], ends], axis=1))
    coarse_out[...] = mm(high, nodal_v[...], 1, 1) + mm(low, nodal_v[...], 1, 1)

    @pl.when(me_g > 0)
    def _():
        to_root(me_g).wait_send()

    @pl.when(me_g == 0)
    def _():
        for k in (1, 2, 15, 3, 4, 5, 6, 7):
            from_root(k).wait_send()

    @pl.when(me_g == 15)
    def _():
        for k in HANDED:
            from_root(k).wait_send()


def body(n_grp, n_dev, elem_stiff, density, owner, agg_slot, par_octant, agg_octant, coarse_map):
    first, lift, signs, nodal = constants()
    row = lambda array: array.reshape(1, -1)
    args = (
        elem_stiff, row(density), row(owner), row(agg_slot), row(par_octant), row(agg_octant), row(coarse_map),
        jnp.asarray(first), jnp.asarray(lift), jnp.asarray(signs), jnp.asarray(nodal),
    )
    dma = pltpu.SemaphoreType.DMA
    level, coarse = pl.pallas_call(
        functools.partial(kernel, n_grp, n_dev),
        out_shape=(pltpu.VMEM((64, 576), F32), pltpu.VMEM((16, 576), F32)),
        in_specs=[pl.BlockSpec(memory_space=pltpu.HBM)] * len(args),
        out_specs=(pl.BlockSpec(memory_space=pltpu.VMEM), pl.BlockSpec(memory_space=pltpu.VMEM)),
        scratch_shapes=[pltpu.VMEM(a.shape, a.dtype) for a in args] + [
            pltpu.VMEM((8, 256, 512), BF16),
            pltpu.VMEM((n_dev, PACK, 128), F32),
            pltpu.VMEM((n_dev, PACK, 128), F32),
            pltpu.VMEM((PACK, 128), F32),
            pltpu.VMEM((n_grp, PACK, 128), F32),
            pltpu.VMEM((PACK, 128), F32),
            dma((9,)), dma((1,)), dma((2,)), dma((n_dev,)), dma((n_dev,)),
            dma((1,)), dma((n_grp,)), dma((n_grp,)), dma((1,)),
        ],
        compiler_params=pltpu.CompilerParams(
            collective_id=0, has_side_effects=True, vmem_limit_bytes=63 * 1024 * 1024
        ),
    )(*args)
    return level.T, coarse.T


def solution(mesh):
    split = P(("grp", "dev"))
    return jax.shard_map(
        functools.partial(body, mesh.shape["grp"], mesh.shape["dev"]),
        mesh=mesh,
        in_specs=(P(None, ("grp", "dev")), split, P(("grp", "dev"), None), split, split, split, split),
        out_specs=(P(None, ("grp", "dev")), P(None, "dev")),
        check_vma=False,
    )
```

```python
import functools

import jax
import jax.numpy as jnp
import ml_dtypes
import numpy as np
from jax import lax
from jax.experimental import pallas as pl
from jax.experimental.pallas import tpu as pltpu
from jax.sharding import PartitionSpec as P

MESH = pl.DeviceIdType.MESH
F32, BF16 = jnp.float32, jnp.bfloat16
MODES = 300
CODE = 300
COLS = 304
WIDE = 384
KEEP = ((0, 384), (400, 432), (448, 480), (496, 528), (544, 576))
SLOTS = 16
FAR_FIRST = sorted(
    [(dx, dy, dc) for dx in range(4) for dy in range(4) for dc in range(2) if dx + dy + dc],
    key=lambda step: -(min(step[0], 4 - step[0]) + min(step[1], 4 - step[1])),
)
HANDED = (8, 9, 10, 11, 12, 13, 14)
PACK = 40


def prolong_np():
    table = np.zeros((8, 24, 24))
    for octant in range(8):
        for child in range(8):
            for corner in range(8):
                value = 1.0
                for bit in range(3):
                    place = (((octant >> bit) & 1) + ((child >> bit) & 1)) / 2.0
                    value *= place if (corner >> bit) & 1 else 1.0 - place
                for comp in range(3):
                    table[octant, child * 3 + comp, corner * 3 + comp] = value
    return table


def constants():
    table = prolong_np()
    axis = np.array([[1.0, -1.0], [1.0, 1.0]])
    basis = np.kron(np.kron(np.kron(axis, axis), axis), np.eye(3))
    pairs = [(k, l) for k in range(24) for l in range(k, 24)]
    ks, ls = np.array([p[0] for p in pairs]), np.array([p[1] for p in pairs])
    kept = np.concatenate([np.arange(a, b) for a, b in KEEP])
    row_i, row_j = kept // 24, kept % 24
    used = row_i <= row_j
    off = (row_i != row_j)[None, :]
    first = np.zeros((8, COLS, kept.size))
    for octant in range(8):
        modes = table[octant] @ basis
        term = modes[row_i][:, ks].T * modes[row_j][:, ls].T
        swap = modes[row_j][:, ks].T * modes[row_i][:, ls].T
        first[octant, :MODES] = np.where(used[None, :], term + off * swap, 0.0)
    step = np.linalg.inv(basis) @ table[7] @ basis
    lift = np.zeros((WIDE, WIDE))
    lift[:MODES, :MODES] = step[ks][:, ks].T * step[ls][:, ls].T + (ks != ls)[None, :] * (step[ls][:, ks].T * step[ks][:, ls].T)
    signs = np.zeros((WIDE, 8))
    parity = (ks // 3) ^ (ls // 3)
    for octant in range(8):
        sign = np.ones(MODES)
        for bit in range(3):
            sign *= np.where((parity >> bit) & 1, 1.0 if (octant >> bit) & 1 else -1.0, 1.0)
        signs[:MODES, octant] = sign
    nodal = np.zeros((576, WIDE))
    a, b = np.arange(576) // 24, np.arange(576) % 24
    nodal[:, :MODES] = (basis[a][:, ks] * basis[b][:, ls] + (ks != ls)[None, :] * basis[a][:, ls] * basis[b][:, ks]) / 64.0
    cast = lambda array: np.asarray(array).astype(ml_dtypes.bfloat16)
    return cast(first), cast(lift), cast(signs), cast(nodal)


def mm(left, right, left_dim=1, right_dim=0):
    return lax.dot_general(left, right, (((left_dim,), (right_dim,)), ((), ())), preferred_element_type=F32)


def iota(shape, dim):
    return lax.broadcasted_iota(jnp.int32, shape, dim)


def halves(value):
    high = value.astype(BF16)
    return high, (value - high.astype(F32)).astype(BF16)


def ones_where(mask):
    return jnp.where(mask, 1.0, 0.0).astype(BF16)


def kernel(
    n_grp, n_dev,
    stiff, dens, owner, slot, par_oct, agg_oct, agg_map, first, lift, signs, nodal,
    level_out, coarse_out,
    stiff_v, dens_v, owner_v, slot_v, par_oct_v, agg_oct_v, agg_map_v, first_v, lift_v, signs_v, nodal_v,
    xt, outgo, income, parts, gathered, totals,
    in_sem, first_sem, stiff_sem, send_sem, recv_sem, part_send, part_recv, total_send, total_recv,
):
    me_g, me_d = lax.axis_index("grp"), lax.axis_index("dev")
    blocks = 8

    small = [
        pltpu.make_async_copy(src, dst, in_sem.at[index])
        for index, (src, dst) in enumerate((
            (dens, dens_v), (owner, owner_v), (slot, slot_v), (par_oct, par_oct_v),
            (agg_oct, agg_oct_v), (agg_map, agg_map_v), (signs, signs_v),
        ))
    ]
    lift_load = pltpu.make_async_copy(lift, lift_v, in_sem.at[7])
    nodal_load = pltpu.make_async_copy(nodal, nodal_v, in_sem.at[8])
    first_load = pltpu.make_async_copy(first, first_v, first_sem.at[0])
    stiff_loads = [
        pltpu.make_async_copy(stiff.at[:, pl.ds(1024 * c, 1024)], stiff_v.at[:, pl.ds(1024 * c, 1024)], stiff_sem.at[c])
        for c in range(2)
    ]
    for load in stiff_loads + small + [first_load, lift_load, nodal_load]:
        load.start()

    barrier = pltpu.get_barrier_semaphore()

    def greet_dev(k, _):
        pl.semaphore_signal(barrier, inc=1, device_id={"dev": lax.rem(me_d + k, n_dev)}, device_id_type=MESH)
        return 0

    def greet_grp(k, _):
        pl.semaphore_signal(barrier, inc=1, device_id={"grp": k}, device_id_type=MESH)
        return 0

    lax.fori_loop(1, n_dev, greet_dev, 0)

    @pl.when(me_g == 0)
    def _():
        lax.fori_loop(1, n_grp, greet_grp, 0)

    @pl.when((me_g >= 8) & (me_g <= 14))
    def _():
        greet_grp(15, 0)

    @pl.when(((me_g >= 1) & (me_g <= 7)) | (me_g == 15))
    def _():
        greet_grp(0, 0)

    pos = iota((256, 256), 0)
    perm = ones_where(iota((256, 256), 1) == 8 * (pos % 32) + pos // 32)

    def turn(b):
        lanes = slice(256 * b, 256 * (b + 1))
        block = jnp.concatenate([stiff_v[a:z, lanes] for a, z in KEEP], axis=0)
        rows = mm(perm, block, 1, 1).astype(BF16)
        for o in range(8):
            xt[o, 32 * b:32 * (b + 1), :] = rows[32 * o:32 * (o + 1)]

    for load in stiff_loads + small:
        load.wait()
    for b in range(8):
        turn(b)

    owner_row = owner_v[...]
    hits = iota((n_dev, 256), 0) == owner_row
    before = ones_where(iota((256, 256), 0) < iota((256, 256), 1))
    hits_f = jnp.where(hits, 1.0, 0.0)
    rank = jnp.sum(mm(hits_f.astype(BF16), before) * hits_f, axis=0, keepdims=True)
    place = owner_row * SLOTS + rank.astype(jnp.int32)
    code = slot_v[...].astype(F32) + 1.0

    picks = ones_where(iota((n_dev * SLOTS, 256), 0) == place)

    dens_row = dens_v[...]
    dens_8 = jnp.concatenate([dens_row[:, 256 * b:256 * (b + 1)] for b in range(blocks)], axis=0)
    weight = 0.001 + 0.999 * dens_8 * dens_8 * dens_8
    one = weight.astype(BF16)
    rest = weight - one.astype(F32)
    two = rest.astype(BF16)
    three = (rest - two.astype(F32)).astype(BF16)
    pieces = jnp.concatenate([one.astype(F32), two.astype(F32), three.astype(F32)], axis=0).astype(BF16)
    turned = mm(perm, pieces, 1, 1).astype(BF16)
    spread = ones_where(iota((24, 256), 0) % 8 == iota((24, 256), 1) // 32)
    spread_w = mm(turned, spread)
    own_row = iota((256, 256), 0) % 32 == iota((256, 256), 1) % 32
    weights = jnp.sum(jnp.where(own_row, spread_w, 0.0).reshape(8, 32, 256), axis=1)

    octs = ones_where(iota((8, 256), 0) == par_oct_v[...])
    flips = mm(signs_v[0:COLS, :], octs)

    first_load.wait()
    lift_load.wait()
    parent = None
    for o in range(8):
        term = mm(first_v[o], xt[o], 1, 1) * weights[o:o + 1, :]
        parent = term if parent is None else parent + term

    high, low = halves(parent * flips)
    lift_c = lift_v[0:COLS, 0:COLS]
    sent = (mm(lift_c, high) + mm(lift_c, low)) * flips
    sent = jnp.where(iota((COLS, 256), 0) == CODE, code, sent)
    tail = sent[256:COLS]
    gap = jnp.zeros((16, 256), F32)
    full = jnp.concatenate([sent, gap, tail, gap], axis=0)
    high, low = halves(full)

    chosen = mm(picks, high, 1, 1) + mm(picks, low, 1, 1)
    outgo[:, 0:16, :] = chosen[:, 0:128].reshape(n_dev, 16, 128)
    outgo[:, 16:32, :] = chosen[:, 128:256].reshape(n_dev, 16, 128)
    ends = chosen[:, 256:384].reshape(n_dev, 2, 8, 128)
    outgo[:, 32:40, :] = jnp.where(iota((n_dev, 8, 128), 2) < 64, ends[:, 0], ends[:, 1])

    @pl.when((me_g == 0) | (me_g == 15))
    def _():
        pl.semaphore_wait(barrier, n_dev - 1 + 8)

    @pl.when((me_g >= 1) & (me_g <= 14))
    def _():
        pl.semaphore_wait(barrier, n_dev)

    def to_owner(peer):
        return pltpu.make_async_remote_copy(
            src_ref=outgo.at[peer], dst_ref=income.at[me_d], send_sem=send_sem.at[0],
            recv_sem=recv_sem.at[0], device_id={"dev": peer}, device_id_type=MESH,
        )

    every_owner = pltpu.make_async_remote_copy(
        src_ref=outgo.at[pl.ds(0, n_dev - 1)], dst_ref=income.at[pl.ds(0, n_dev - 1)], send_sem=send_sem.at[0],
        recv_sem=recv_sem.at[0], device_id={"dev": lax.rem(me_d + 1, n_dev)}, device_id_type=MESH,
    )

    x, y, core = lax.div(me_d, 8), lax.rem(lax.div(me_d, 2), 4), lax.rem(me_d, 2)
    for dx, dy, dc in FAR_FIRST:
        to_owner((lax.rem(x + dx, 4) * 4 + lax.rem(y + dy, 4)) * 2 + lax.rem(core + dc, 2)).start()
    income[me_d] = outgo[me_d]

    octs = ones_where(iota((8, 64), 0) == agg_oct_v[...])
    agg_flips = mm(octs, signs_v[...], 0, 1)
    sums = ones_where(iota((16, 64), 0) == agg_map_v[...])
    nodal_load.wait()

    every_owner.wait_recv()

    lane = iota((8, 128), 1)
    code_at = ones_where(lane == CODE - 256 + 64 * iota((8, 128), 0))
    packed = income[:, 32:40, :].reshape(n_dev * 8, 128)
    codes = mm(code_at, packed.astype(BF16), 1, 1).astype(jnp.int32)
    level = []
    for h in range(2):
        into = ones_where(iota((64, n_dev * 8), 0) == codes[h:h + 1, :] - 1)
        wide = jnp.concatenate([
            income[:, 8 * h:8 * h + 8, :].reshape(n_dev * 8, 128),
            income[:, 16 + 8 * h:24 + 8 * h, :].reshape(n_dev * 8, 128),
            packed,
        ], axis=1)
        high, low = halves(wide)
        level.append(mm(into, high) + mm(into, low))
    ends = level[0][:, 256:] + pltpu.roll(level[1][:, 256:], 64, 1)
    ends = jnp.where(iota((64, 128), 1) < MODES - 256, ends, 0.0)
    level = jnp.concatenate([level[0][:, :256] + level[1][:, :256], ends], axis=1)

    both = jnp.concatenate(halves(level * agg_flips), axis=0)
    lifted = mm(both, lift_v[...], 1, 1)
    high, low = halves((lifted[0:64] + lifted[64:128]) * agg_flips)
    share = mm(sums, high) + mm(sums, low)
    parts[0:16, :] = share[:, 0:128]
    parts[16:32, :] = share[:, 128:256]
    parts[32:40, :] = jnp.where(iota((8, 128), 1) < 64, share[0:8, 256:384], pltpu.roll(share[8:16, 256:384], 64, 1))

    def to_root(source):
        return pltpu.make_async_remote_copy(
            src_ref=parts, dst_ref=gathered.at[source], send_sem=part_send.at[0],
            recv_sem=part_recv.at[0], device_id={"grp": 0}, device_id_type=MESH,
        )

    def from_root(target):
        return pltpu.make_async_remote_copy(
            src_ref=totals, dst_ref=totals, send_sem=total_send.at[target],
            recv_sem=total_recv.at[0], device_id={"grp": target}, device_id_type=MESH,
        )

    @pl.when(me_g > 0)
    def _():
        to_root(me_g).start()

    high, low = halves(level)
    level_out[...] = mm(high, nodal_v[...], 1, 1) + mm(low, nodal_v[...], 1, 1)
    every_owner.wait_send()

    @pl.when(me_g == 0)
    def _():
        pltpu.make_async_remote_copy(
            src_ref=gathered.at[pl.ds(1, n_grp - 1)], dst_ref=gathered.at[pl.ds(1, n_grp - 1)], send_sem=part_send.at[0],
            recv_sem=part_recv.at[0], device_id={"grp": 1}, device_id_type=MESH,
        ).wait_recv()
        sums = [parts[...]] + [gathered[k] for k in range(1, n_grp)]
        while len(sums) > 1:
            sums = [sums[k] + sums[k + 1] for k in range(0, len(sums), 2)]
        totals[...] = sums[0]
        for k in (1, 2, 15, 3, 4, 5, 6, 7):
            from_root(k).start()

    @pl.when(me_g > 0)
    def _():
        from_root(me_g).wait_recv()

    @pl.when(me_g == 15)
    def _():
        for k in HANDED:
            from_root(k).start()

    ends = totals[32:40, :]
    ends = jnp.concatenate([ends, pltpu.roll(ends, 64, 1)], axis=0)
    high, low = halves(jnp.concatenate([totals[0:16, :], totals[16:32, :], ends], axis=1))
    coarse_out[...] = mm(high, nodal_v[...], 1, 1) + mm(low, nodal_v[...], 1, 1)

    @pl.when(me_g > 0)
    def _():
        to_root(me_g).wait_send()

    @pl.when(me_g == 0)
    def _():
        for k in (1, 2, 15, 3, 4, 5, 6, 7):
            from_root(k).wait_send()

    @pl.when(me_g == 15)
    def _():
        for k in HANDED:
            from_root(k).wait_send()


def body(n_grp, n_dev, elem_stiff, density, owner, agg_slot, par_octant, agg_octant, coarse_map):
    first, lift, signs, nodal = constants()
    row = lambda array: array.reshape(1, -1)
    args = (
        elem_stiff, row(density), row(owner), row(agg_slot), row(par_octant), row(agg_octant), row(coarse_map),
        jnp.asarray(first), jnp.asarray(lift), jnp.asarray(signs), jnp.asarray(nodal),
    )
    dma = pltpu.SemaphoreType.DMA
    level, coarse = pl.pallas_call(
        functools.partial(kernel, n_grp, n_dev),
        out_shape=(pltpu.VMEM((64, 576), F32), pltpu.VMEM((16, 576), F32)),
        in_specs=[pl.BlockSpec(memory_space=pltpu.HBM)] * len(args),
        out_specs=(pl.BlockSpec(memory_space=pltpu.VMEM), pl.BlockSpec(memory_space=pltpu.VMEM)),
        scratch_shapes=[pltpu.VMEM(a.shape, a.dtype) for a in args] + [
            pltpu.VMEM((8, 256, 512), BF16),
            pltpu.VMEM((n_dev, PACK, 128), F32),
            pltpu.VMEM((n_dev, PACK, 128), F32),
            pltpu.VMEM((PACK, 128), F32),
            pltpu.VMEM((n_grp, PACK, 128), F32),
            pltpu.VMEM((PACK, 128), F32),
            dma((9,)), dma((1,)), dma((2,)), dma((1,)), dma((1,)),
            dma((1,)), dma((1,)), dma((n_grp,)), dma((1,)),
        ],
        compiler_params=pltpu.CompilerParams(
            collective_id=0, has_side_effects=True, vmem_limit_bytes=63 * 1024 * 1024
        ),
    )(*args)
    return level.T, coarse.T


def solution(mesh):
    split = P(("grp", "dev"))
    return jax.shard_map(
        functools.partial(body, mesh.shape["grp"], mesh.shape["dev"]),
        mesh=mesh,
        in_specs=(P(None, ("grp", "dev")), split, P(("grp", "dev"), None), split, split, split, split),
        out_specs=(P(None, ("grp", "dev")), P(None, "dev")),
        check_vma=False,
    )
```

```python
import functools

import jax
import jax.numpy as jnp
import ml_dtypes
import numpy as np
from jax import lax
from jax.experimental import pallas as pl
from jax.experimental.pallas import tpu as pltpu
from jax.sharding import PartitionSpec as P

MESH = pl.DeviceIdType.MESH
F32, BF16 = jnp.float32, jnp.bfloat16
MODES = 300
CODE = 300
COLS = 304
WIDE = 384
KEEP = ((0, 384), (400, 432), (448, 480), (496, 528), (544, 576))
SLOTS = 16
FAR_FIRST = sorted(
    [(dx, dy, dc) for dx in range(4) for dy in range(4) for dc in range(2) if dx + dy + dc],
    key=lambda step: -(min(step[0], 4 - step[0]) + min(step[1], 4 - step[1])),
)
HANDED = (8, 9, 10, 11, 12, 13, 14)
PACK = 40


def prolong_np():
    table = np.zeros((8, 24, 24))
    for octant in range(8):
        for child in range(8):
            for corner in range(8):
                value = 1.0
                for bit in range(3):
                    place = (((octant >> bit) & 1) + ((child >> bit) & 1)) / 2.0
                    value *= place if (corner >> bit) & 1 else 1.0 - place
                for comp in range(3):
                    table[octant, child * 3 + comp, corner * 3 + comp] = value
    return table


def constants():
    table = prolong_np()
    axis = np.array([[1.0, -1.0], [1.0, 1.0]])
    basis = np.kron(np.kron(np.kron(axis, axis), axis), np.eye(3))
    pairs = [(k, l) for k in range(24) for l in range(k, 24)]
    ks, ls = np.array([p[0] for p in pairs]), np.array([p[1] for p in pairs])
    kept = np.concatenate([np.arange(a, b) for a, b in KEEP])
    row_i, row_j = kept // 24, kept % 24
    used = row_i <= row_j
    off = (row_i != row_j)[None, :]
    first = np.zeros((8, COLS, kept.size))
    for octant in range(8):
        modes = table[octant] @ basis
        term = modes[row_i][:, ks].T * modes[row_j][:, ls].T
        swap = modes[row_j][:, ks].T * modes[row_i][:, ls].T
        first[octant, :MODES] = np.where(used[None, :], term + off * swap, 0.0)
    step = np.linalg.inv(basis) @ table[7] @ basis
    lift = np.zeros((WIDE, WIDE))
    lift[:MODES, :MODES] = step[ks][:, ks].T * step[ls][:, ls].T + (ks != ls)[None, :] * (step[ls][:, ks].T * step[ks][:, ls].T)
    signs = np.zeros((WIDE, 8))
    parity = (ks // 3) ^ (ls // 3)
    for octant in range(8):
        sign = np.ones(MODES)
        for bit in range(3):
            sign *= np.where((parity >> bit) & 1, 1.0 if (octant >> bit) & 1 else -1.0, 1.0)
        signs[:MODES, octant] = sign
    nodal = np.zeros((576, WIDE))
    a, b = np.arange(576) // 24, np.arange(576) % 24
    nodal[:, :MODES] = (basis[a][:, ks] * basis[b][:, ls] + (ks != ls)[None, :] * basis[a][:, ls] * basis[b][:, ks]) / 64.0
    cast = lambda array: np.asarray(array).astype(ml_dtypes.bfloat16)
    return cast(first), cast(lift), cast(signs), cast(nodal)


def mm(left, right, left_dim=1, right_dim=0):
    return lax.dot_general(left, right, (((left_dim,), (right_dim,)), ((), ())), preferred_element_type=F32)


def iota(shape, dim):
    return lax.broadcasted_iota(jnp.int32, shape, dim)


def halves(value):
    high = value.astype(BF16)
    return high, (value - high.astype(F32)).astype(BF16)


def ones_where(mask):
    return jnp.where(mask, 1.0, 0.0).astype(BF16)


def kernel(
    n_grp, n_dev,
    stiff, dens, owner, slot, par_oct, agg_oct, agg_map, first, lift, signs, nodal,
    level_out, coarse_out,
    stiff_v, dens_v, owner_v, slot_v, par_oct_v, agg_oct_v, agg_map_v, first_v, lift_v, signs_v, nodal_v,
    xt, outgo, income, parts, gathered, totals,
    in_sem, first_sem, stiff_sem, send_sem, recv_sem, part_send, part_recv, total_send, total_recv,
):
    me_g, me_d = lax.axis_index("grp"), lax.axis_index("dev")
    blocks = 8

    small = [
        pltpu.make_async_copy(src, dst, in_sem.at[index])
        for index, (src, dst) in enumerate((
            (dens, dens_v), (owner, owner_v), (slot, slot_v), (par_oct, par_oct_v),
            (agg_oct, agg_oct_v), (agg_map, agg_map_v), (signs, signs_v),
        ))
    ]
    lift_load = pltpu.make_async_copy(lift, lift_v, in_sem.at[7])
    nodal_load = pltpu.make_async_copy(nodal, nodal_v, in_sem.at[8])
    first_load = pltpu.make_async_copy(first, first_v, first_sem.at[0])
    stiff_loads = [
        pltpu.make_async_copy(stiff.at[:, pl.ds(1024 * c, 1024)], stiff_v.at[:, pl.ds(1024 * c, 1024)], stiff_sem.at[c])
        for c in range(2)
    ]
    for load in stiff_loads + small + [first_load, lift_load, nodal_load]:
        load.start()

    barrier = pltpu.get_barrier_semaphore()

    def greet_dev(k, _):
        pl.semaphore_signal(barrier, inc=1, device_id={"dev": lax.rem(me_d + k, n_dev)}, device_id_type=MESH)
        return 0

    def greet_grp(k, _):
        pl.semaphore_signal(barrier, inc=1, device_id={"grp": k}, device_id_type=MESH)
        return 0

    lax.fori_loop(1, n_dev, greet_dev, 0)

    @pl.when(me_g == 0)
    def _():
        lax.fori_loop(1, n_grp, greet_grp, 0)

    @pl.when((me_g >= 8) & (me_g <= 14))
    def _():
        greet_grp(15, 0)

    @pl.when(((me_g >= 1) & (me_g <= 7)) | (me_g == 15))
    def _():
        greet_grp(0, 0)

    pos = iota((256, 256), 0)
    perm = ones_where(iota((256, 256), 1) == 8 * (pos % 32) + pos // 32)

    def turn(b):
        lanes = slice(256 * b, 256 * (b + 1))
        block = jnp.concatenate([stiff_v[a:z, lanes] for a, z in KEEP], axis=0)
        rows = mm(perm, block, 1, 1).astype(BF16)
        for o in range(8):
            xt[o, 32 * b:32 * (b + 1), :] = rows[32 * o:32 * (o + 1)]

    for load in stiff_loads + small:
        load.wait()
    for b in range(8):
        turn(b)

    owner_row = owner_v[...]
    hits = iota((n_dev, 256), 0) == owner_row
    before = ones_where(iota((256, 256), 0) < iota((256, 256), 1))
    hits_f = jnp.where(hits, 1.0, 0.0)
    rank = jnp.sum(mm(hits_f.astype(BF16), before) * hits_f, axis=0, keepdims=True)
    place = owner_row * SLOTS + rank.astype(jnp.int32)
    code = slot_v[...].astype(F32) + 1.0

    picks = ones_where(iota((n_dev * SLOTS, 256), 0) == place)

    dens_row = dens_v[...]
    dens_8 = jnp.concatenate([dens_row[:, 256 * b:256 * (b + 1)] for b in range(blocks)], axis=0)
    weight = 0.001 + 0.999 * dens_8 * dens_8 * dens_8
    one = weight.astype(BF16)
    rest = weight - one.astype(F32)
    two = rest.astype(BF16)
    three = (rest - two.astype(F32)).astype(BF16)
    pieces = jnp.concatenate([one.astype(F32), two.astype(F32), three.astype(F32)], axis=0).astype(BF16)
    turned = mm(perm, pieces, 1, 1).astype(BF16)
    spread = ones_where(iota((24, 256), 0) % 8 == iota((24, 256), 1) // 32)
    spread_w = mm(turned, spread)
    own_row = iota((256, 256), 0) % 32 == iota((256, 256), 1) % 32
    weights = jnp.sum(jnp.where(own_row, spread_w, 0.0).reshape(8, 32, 256), axis=1)

    octs = ones_where(iota((8, 256), 0) == par_oct_v[...])
    flips = mm(signs_v[0:COLS, :], octs)

    first_load.wait()
    lift_load.wait()
    parent = None
    for o in range(8):
        term = mm(first_v[o], xt[o], 1, 1) * weights[o:o + 1, :]
        parent = term if parent is None else parent + term

    high, low = halves(parent * flips)
    lift_c = lift_v[0:COLS, 0:COLS]
    sent = (mm(lift_c, high) + mm(lift_c, low)) * flips
    sent = jnp.where(iota((COLS, 256), 0) == CODE, code, sent)
    tail = sent[256:COLS]
    gap = jnp.zeros((16, 256), F32)
    full = jnp.concatenate([sent, gap, tail, gap], axis=0)
    high, low = halves(full)

    chosen = mm(jnp.concatenate([picks, picks], axis=1), jnp.concatenate([high, low], axis=1), 1, 1)
    outgo[:, 0:16, :] = chosen[:, 0:128].reshape(n_dev, 16, 128)
    outgo[:, 16:32, :] = chosen[:, 128:256].reshape(n_dev, 16, 128)
    ends = chosen[:, 256:384].reshape(n_dev, 2, 8, 128)
    outgo[:, 32:40, :] = jnp.where(iota((n_dev, 8, 128), 2) < 64, ends[:, 0], ends[:, 1])

    @pl.when((me_g == 0) | (me_g == 15))
    def _():
        pl.semaphore_wait(barrier, n_dev - 1 + 8)

    @pl.when((me_g >= 1) & (me_g <= 14))
    def _():
        pl.semaphore_wait(barrier, n_dev)

    def to_owner(peer):
        return pltpu.make_async_remote_copy(
            src_ref=outgo.at[peer], dst_ref=income.at[me_d], send_sem=send_sem.at[0],
            recv_sem=recv_sem.at[0], device_id={"dev": peer}, device_id_type=MESH,
        )

    every_owner = pltpu.make_async_remote_copy(
        src_ref=outgo.at[pl.ds(0, n_dev - 1)], dst_ref=income.at[pl.ds(0, n_dev - 1)], send_sem=send_sem.at[0],
        recv_sem=recv_sem.at[0], device_id={"dev": lax.rem(me_d + 1, n_dev)}, device_id_type=MESH,
    )

    x, y, core = lax.div(me_d, 8), lax.rem(lax.div(me_d, 2), 4), lax.rem(me_d, 2)
    for dx, dy, dc in FAR_FIRST:
        to_owner((lax.rem(x + dx, 4) * 4 + lax.rem(y + dy, 4)) * 2 + lax.rem(core + dc, 2)).start()
    income[me_d] = outgo[me_d]

    octs = ones_where(iota((8, 64), 0) == agg_oct_v[...])
    agg_flips = mm(octs, signs_v[...], 0, 1)
    sums = ones_where(iota((16, 64), 0) == agg_map_v[...])
    nodal_load.wait()

    every_owner.wait_recv()

    lane = iota((8, 128), 1)
    code_at = ones_where(lane == CODE - 256 + 64 * iota((8, 128), 0))
    packed = income[:, 32:40, :].reshape(n_dev * 8, 128)
    codes = mm(code_at, packed.astype(BF16), 1, 1).astype(jnp.int32)
    level = []
    for h in range(2):
        into = ones_where(iota((64, n_dev * 8), 0) == codes[h:h + 1, :] - 1)
        wide = jnp.concatenate([
            income[:, 8 * h:8 * h + 8, :].reshape(n_dev * 8, 128),
            income[:, 16 + 8 * h:24 + 8 * h, :].reshape(n_dev * 8, 128),
            packed,
        ], axis=1)
        high, low = halves(wide)
        level.append(mm(jnp.concatenate([into, into], axis=1), jnp.concatenate([high, low], axis=0)))
    ends = level[0][:, 256:] + pltpu.roll(level[1][:, 256:], 64, 1)
    ends = jnp.where(iota((64, 128), 1) < MODES - 256, ends, 0.0)
    level = jnp.concatenate([level[0][:, :256] + level[1][:, :256], ends], axis=1)

    both = jnp.concatenate(halves(level * agg_flips), axis=0)
    lifted = mm(both, lift_v[...], 1, 1)
    high, low = halves((lifted[0:64] + lifted[64:128]) * agg_flips)
    share = mm(jnp.concatenate([sums, sums], axis=1), jnp.concatenate([high, low], axis=0))
    parts[0:16, :] = share[:, 0:128]
    parts[16:32, :] = share[:, 128:256]
    parts[32:40, :] = jnp.where(iota((8, 128), 1) < 64, share[0:8, 256:384], pltpu.roll(share[8:16, 256:384], 64, 1))

    def to_root(source):
        return pltpu.make_async_remote_copy(
            src_ref=parts, dst_ref=gathered.at[source], send_sem=part_send.at[0],
            recv_sem=part_recv.at[0], device_id={"grp": 0}, device_id_type=MESH,
        )

    def from_root(target):
        return pltpu.make_async_remote_copy(
            src_ref=totals, dst_ref=totals, send_sem=total_send.at[target],
            recv_sem=total_recv.at[0], device_id={"grp": target}, device_id_type=MESH,
        )

    @pl.when(me_g > 0)
    def _():
        to_root(me_g).start()

    high, low = halves(level)
    both = mm(jnp.concatenate([high, low], axis=0), nodal_v[...], 1, 1)
    level_out[...] = both[0:64] + both[64:128]
    every_owner.wait_send()

    @pl.when(me_g == 0)
    def _():
        pltpu.make_async_remote_copy(
            src_ref=gathered.at[pl.ds(1, n_grp - 1)], dst_ref=gathered.at[pl.ds(1, n_grp - 1)], send_sem=part_send.at[0],
            recv_sem=part_recv.at[0], device_id={"grp": 1}, device_id_type=MESH,
        ).wait_recv()
        sums = [parts[...]] + [gathered[k] for k in range(1, n_grp)]
        while len(sums) > 1:
            sums = [sums[k] + sums[k + 1] for k in range(0, len(sums), 2)]
        totals[...] = sums[0]
        for k in (1, 2, 15, 3, 4, 5, 6, 7):
            from_root(k).start()

    @pl.when(me_g > 0)
    def _():
        from_root(me_g).wait_recv()

    @pl.when(me_g == 15)
    def _():
        for k in HANDED:
            from_root(k).start()

    ends = totals[32:40, :]
    ends = jnp.concatenate([ends, pltpu.roll(ends, 64, 1)], axis=0)
    high, low = halves(jnp.concatenate([totals[0:16, :], totals[16:32, :], ends], axis=1))
    both = mm(jnp.concatenate([high, low], axis=0), nodal_v[...], 1, 1)
    coarse_out[...] = both[0:16] + both[16:32]

    @pl.when(me_g > 0)
    def _():
        to_root(me_g).wait_send()

    @pl.when(me_g == 0)
    def _():
        for k in (1, 2, 15, 3, 4, 5, 6, 7):
            from_root(k).wait_send()

    @pl.when(me_g == 15)
    def _():
        for k in HANDED:
            from_root(k).wait_send()


def body(n_grp, n_dev, elem_stiff, density, owner, agg_slot, par_octant, agg_octant, coarse_map):
    first, lift, signs, nodal = constants()
    row = lambda array: array.reshape(1, -1)
    args = (
        elem_stiff, row(density), row(owner), row(agg_slot), row(par_octant), row(agg_octant), row(coarse_map),
        jnp.asarray(first), jnp.asarray(lift), jnp.asarray(signs), jnp.asarray(nodal),
    )
    dma = pltpu.SemaphoreType.DMA
    level, coarse = pl.pallas_call(
        functools.partial(kernel, n_grp, n_dev),
        out_shape=(pltpu.VMEM((64, 576), F32), pltpu.VMEM((16, 576), F32)),
        in_specs=[pl.BlockSpec(memory_space=pltpu.HBM)] * len(args),
        out_specs=(pl.BlockSpec(memory_space=pltpu.VMEM), pl.BlockSpec(memory_space=pltpu.VMEM)),
        scratch_shapes=[pltpu.VMEM(a.shape, a.dtype) for a in args] + [
            pltpu.VMEM((8, 256, 512), BF16),
            pltpu.VMEM((n_dev, PACK, 128), F32),
            pltpu.VMEM((n_dev, PACK, 128), F32),
            pltpu.VMEM((PACK, 128), F32),
            pltpu.VMEM((n_grp, PACK, 128), F32),
            pltpu.VMEM((PACK, 128), F32),
            dma((9,)), dma((1,)), dma((2,)), dma((1,)), dma((1,)),
            dma((1,)), dma((1,)), dma((n_grp,)), dma((1,)),
        ],
        compiler_params=pltpu.CompilerParams(
            collective_id=0, has_side_effects=True, vmem_limit_bytes=63 * 1024 * 1024
        ),
    )(*args)
    return level.T, coarse.T


def solution(mesh):
    split = P(("grp", "dev"))
    return jax.shard_map(
        functools.partial(body, mesh.shape["grp"], mesh.shape["dev"]),
        mesh=mesh,
        in_specs=(P(None, ("grp", "dev")), split, P(("grp", "dev"), None), split, split, split, split),
        out_specs=(P(None, ("grp", "dev")), P(None, "dev")),
        check_vma=False,
    )
```

```python
import functools

import jax
import jax.numpy as jnp
import ml_dtypes
import numpy as np
from jax import lax
from jax.experimental import pallas as pl
from jax.experimental.pallas import tpu as pltpu
from jax.sharding import PartitionSpec as P

MESH = pl.DeviceIdType.MESH
F32, BF16 = jnp.float32, jnp.bfloat16
MODES = 300
CODE = 300
COLS = 304
WIDE = 384
KEEP = ((0, 384), (400, 432), (448, 480), (496, 528), (544, 576))
SLOTS = 16
FAR_FIRST = sorted(
    [(dx, dy, dc) for dx in range(4) for dy in range(4) for dc in range(2) if dx + dy + dc],
    key=lambda step: -(min(step[0], 4 - step[0]) + min(step[1], 4 - step[1])),
)
HANDED = (8, 9, 10, 11, 12, 13, 14)
PACK = 40


def prolong_np():
    table = np.zeros((8, 24, 24))
    for octant in range(8):
        for child in range(8):
            for corner in range(8):
                value = 1.0
                for bit in range(3):
                    place = (((octant >> bit) & 1) + ((child >> bit) & 1)) / 2.0
                    value *= place if (corner >> bit) & 1 else 1.0 - place
                for comp in range(3):
                    table[octant, child * 3 + comp, corner * 3 + comp] = value
    return table


def constants():
    table = prolong_np()
    axis = np.array([[1.0, -1.0], [1.0, 1.0]])
    basis = np.kron(np.kron(np.kron(axis, axis), axis), np.eye(3))
    pairs = [(k, l) for k in range(24) for l in range(k, 24)]
    ks, ls = np.array([p[0] for p in pairs]), np.array([p[1] for p in pairs])
    kept = np.concatenate([np.arange(a, b) for a, b in KEEP])
    row_i, row_j = kept // 24, kept % 24
    used = row_i <= row_j
    off = (row_i != row_j)[None, :]
    first = np.zeros((8, COLS, kept.size))
    for octant in range(8):
        modes = table[octant] @ basis
        term = modes[row_i][:, ks].T * modes[row_j][:, ls].T
        swap = modes[row_j][:, ks].T * modes[row_i][:, ls].T
        first[octant, :MODES] = np.where(used[None, :], term + off * swap, 0.0) / 64.0
    step = np.linalg.inv(basis) @ table[7] @ basis
    lift = np.zeros((WIDE, WIDE))
    lift[:MODES, :MODES] = step[ks][:, ks].T * step[ls][:, ls].T + (ks != ls)[None, :] * (step[ls][:, ks].T * step[ks][:, ls].T)
    signs = np.zeros((WIDE, 8))
    parity = (ks // 3) ^ (ls // 3)
    for octant in range(8):
        sign = np.ones(MODES)
        for bit in range(3):
            sign *= np.where((parity >> bit) & 1, 1.0 if (octant >> bit) & 1 else -1.0, 1.0)
        signs[:MODES, octant] = sign
    nodal = np.zeros((576, WIDE))
    a, b = np.arange(576) // 24, np.arange(576) % 24
    nodal[:, :MODES] = basis[a][:, ks] * basis[b][:, ls] + (ks != ls)[None, :] * basis[a][:, ls] * basis[b][:, ks]
    cast = lambda array: np.asarray(array).astype(ml_dtypes.bfloat16)
    return cast(first), cast(lift), cast(signs), cast(nodal)


def mm(left, right, left_dim=1, right_dim=0):
    return lax.dot_general(left, right, (((left_dim,), (right_dim,)), ((), ())), preferred_element_type=F32)


def iota(shape, dim):
    return lax.broadcasted_iota(jnp.int32, shape, dim)


def halves(value):
    high = value.astype(BF16)
    return high, (value - high.astype(F32)).astype(BF16)


def ones_where(mask):
    return jnp.where(mask, 1.0, 0.0).astype(BF16)


def kernel(
    n_grp, n_dev,
    stiff, dens, owner, slot, par_oct, agg_oct, agg_map, first, lift, signs, nodal,
    level_out, coarse_out,
    stiff_v, dens_v, owner_v, slot_v, par_oct_v, agg_oct_v, agg_map_v, first_v, lift_v, signs_v, nodal_v,
    xt, outgo, income, parts, gathered, totals,
    in_sem, first_sem, stiff_sem, send_sem, recv_sem, part_send, part_recv, total_send, total_recv,
):
    me_g, me_d = lax.axis_index("grp"), lax.axis_index("dev")
    blocks = 8

    small = [
        pltpu.make_async_copy(src, dst, in_sem.at[index])
        for index, (src, dst) in enumerate((
            (dens, dens_v), (owner, owner_v), (slot, slot_v), (par_oct, par_oct_v),
            (agg_oct, agg_oct_v), (agg_map, agg_map_v), (signs, signs_v),
        ))
    ]
    lift_load = pltpu.make_async_copy(lift, lift_v, in_sem.at[7])
    nodal_load = pltpu.make_async_copy(nodal, nodal_v, in_sem.at[8])
    first_load = pltpu.make_async_copy(first, first_v, first_sem.at[0])
    stiff_loads = [
        pltpu.make_async_copy(stiff.at[:, pl.ds(1024 * c, 1024)], stiff_v.at[:, pl.ds(1024 * c, 1024)], stiff_sem.at[c])
        for c in range(2)
    ]
    for load in stiff_loads + small + [first_load, lift_load, nodal_load]:
        load.start()

    barrier = pltpu.get_barrier_semaphore()

    def greet_dev(k, _):
        pl.semaphore_signal(barrier, inc=1, device_id={"dev": lax.rem(me_d + k, n_dev)}, device_id_type=MESH)
        return 0

    def greet_grp(k, _):
        pl.semaphore_signal(barrier, inc=1, device_id={"grp": k}, device_id_type=MESH)
        return 0

    lax.fori_loop(1, n_dev, greet_dev, 0)

    @pl.when(me_g == 0)
    def _():
        lax.fori_loop(1, n_grp, greet_grp, 0)

    @pl.when((me_g >= 8) & (me_g <= 14))
    def _():
        greet_grp(15, 0)

    @pl.when(((me_g >= 1) & (me_g <= 7)) | (me_g == 15))
    def _():
        greet_grp(0, 0)

    pos = iota((256, 256), 0)
    perm = ones_where(iota((256, 256), 1) == 8 * (pos % 32) + pos // 32)

    def turn(b):
        lanes = slice(256 * b, 256 * (b + 1))
        block = jnp.concatenate([stiff_v[a:z, lanes] for a, z in KEEP], axis=0)
        rows = mm(perm, block, 1, 1).astype(BF16)
        for o in range(8):
            xt[o, 32 * b:32 * (b + 1), :] = rows[32 * o:32 * (o + 1)]

    for load in stiff_loads + small:
        load.wait()
    for b in range(8):
        turn(b)

    owner_row = owner_v[...]
    hits = iota((n_dev, 256), 0) == owner_row
    before = ones_where(iota((256, 256), 0) < iota((256, 256), 1))
    hits_f = jnp.where(hits, 1.0, 0.0)
    rank = jnp.sum(mm(hits_f.astype(BF16), before) * hits_f, axis=0, keepdims=True)
    place = owner_row * SLOTS + rank.astype(jnp.int32)
    code = slot_v[...].astype(F32) + 1.0

    picks = ones_where(iota((n_dev * SLOTS, 256), 0) == place)

    dens_row = dens_v[...]
    dens_8 = jnp.concatenate([dens_row[:, 256 * b:256 * (b + 1)] for b in range(blocks)], axis=0)
    weight = 0.001 + 0.999 * dens_8 * dens_8 * dens_8
    one = weight.astype(BF16)
    rest = weight - one.astype(F32)
    two = rest.astype(BF16)
    three = (rest - two.astype(F32)).astype(BF16)
    pieces = jnp.concatenate([one.astype(F32), two.astype(F32), three.astype(F32)], axis=0).astype(BF16)
    turned = mm(perm, pieces, 1, 1).astype(BF16)
    spread = ones_where(iota((24, 256), 0) % 8 == iota((24, 256), 1) // 32)
    spread_w = mm(turned, spread)
    own_row = iota((256, 256), 0) % 32 == iota((256, 256), 1) % 32
    weights = jnp.sum(jnp.where(own_row, spread_w, 0.0).reshape(8, 32, 256), axis=1)

    octs = ones_where(iota((8, 256), 0) == par_oct_v[...])
    flips = mm(signs_v[0:COLS, :], octs)

    first_load.wait()
    lift_load.wait()
    parent = None
    for o in range(8):
        term = mm(first_v[o], xt[o], 1, 1) * weights[o:o + 1, :]
        parent = term if parent is None else parent + term

    high, low = halves(parent * flips)
    lift_c = lift_v[0:COLS, 0:COLS]
    sent = (mm(lift_c, high) + mm(lift_c, low)) * flips
    sent = jnp.where(iota((COLS, 256), 0) == CODE, code, sent)
    tail = sent[256:COLS]
    gap = jnp.zeros((16, 256), F32)
    full = jnp.concatenate([sent, gap, tail, gap], axis=0)
    high, low = halves(full)

    chosen = mm(jnp.concatenate([picks, picks], axis=1), jnp.concatenate([high, low], axis=1), 1, 1)
    outgo[:, 0:16, :] = chosen[:, 0:128].reshape(n_dev, 16, 128)
    outgo[:, 16:32, :] = chosen[:, 128:256].reshape(n_dev, 16, 128)
    ends = chosen[:, 256:384].reshape(n_dev, 2, 8, 128)
    outgo[:, 32:40, :] = jnp.where(iota((n_dev, 8, 128), 2) < 64, ends[:, 0], ends[:, 1])

    @pl.when((me_g == 0) | (me_g == 15))
    def _():
        pl.semaphore_wait(barrier, n_dev - 1 + 8)

    @pl.when((me_g >= 1) & (me_g <= 14))
    def _():
        pl.semaphore_wait(barrier, n_dev)

    def to_owner(peer):
        return pltpu.make_async_remote_copy(
            src_ref=outgo.at[peer], dst_ref=income.at[me_d], send_sem=send_sem.at[0],
            recv_sem=recv_sem.at[0], device_id={"dev": peer}, device_id_type=MESH,
        )

    every_owner = pltpu.make_async_remote_copy(
        src_ref=outgo.at[pl.ds(0, n_dev - 1)], dst_ref=income.at[pl.ds(0, n_dev - 1)], send_sem=send_sem.at[0],
        recv_sem=recv_sem.at[0], device_id={"dev": lax.rem(me_d + 1, n_dev)}, device_id_type=MESH,
    )

    x, y, core = lax.div(me_d, 8), lax.rem(lax.div(me_d, 2), 4), lax.rem(me_d, 2)
    for dx, dy, dc in FAR_FIRST:
        to_owner((lax.rem(x + dx, 4) * 4 + lax.rem(y + dy, 4)) * 2 + lax.rem(core + dc, 2)).start()
    income[me_d] = outgo[me_d]

    octs = ones_where(iota((8, 64), 0) == agg_oct_v[...])
    agg_flips = mm(octs, signs_v[...], 0, 1)
    sums = ones_where(iota((16, 64), 0) == agg_map_v[...])
    nodal_load.wait()

    every_owner.wait_recv()

    lane = iota((8, 128), 1)
    code_at = ones_where(lane == CODE - 256 + 64 * iota((8, 128), 0))
    packed = income[:, 32:40, :].reshape(n_dev * 8, 128)
    codes = mm(code_at, packed.astype(BF16), 1, 1).astype(jnp.int32)
    level = []
    for h in range(2):
        into = ones_where(iota((64, n_dev * 8), 0) == codes[h:h + 1, :] - 1)
        wide = jnp.concatenate([
            income[:, 8 * h:8 * h + 8, :].reshape(n_dev * 8, 128),
            income[:, 16 + 8 * h:24 + 8 * h, :].reshape(n_dev * 8, 128),
            packed,
        ], axis=1)
        high, low = halves(wide)
        level.append(mm(jnp.concatenate([into, into], axis=1), jnp.concatenate([high, low], axis=0)))
    ends = level[0][:, 256:] + pltpu.roll(level[1][:, 256:], 64, 1)
    ends = jnp.where(iota((64, 128), 1) < MODES - 256, ends, 0.0)
    level = jnp.concatenate([level[0][:, :256] + level[1][:, :256], ends], axis=1)

    both = jnp.concatenate(halves(level * agg_flips), axis=0)
    lifted = mm(both, lift_v[...], 1, 1)
    high, low = halves((lifted[0:64] + lifted[64:128]) * agg_flips)
    share = mm(jnp.concatenate([sums, sums], axis=1), jnp.concatenate([high, low], axis=0))
    parts[0:16, :] = share[:, 0:128]
    parts[16:32, :] = share[:, 128:256]
    parts[32:40, :] = jnp.where(iota((8, 128), 1) < 64, share[0:8, 256:384], pltpu.roll(share[8:16, 256:384], 64, 1))

    def to_root(source):
        return pltpu.make_async_remote_copy(
            src_ref=parts, dst_ref=gathered.at[source], send_sem=part_send.at[0],
            recv_sem=part_recv.at[0], device_id={"grp": 0}, device_id_type=MESH,
        )

    def from_root(target):
        return pltpu.make_async_remote_copy(
            src_ref=totals, dst_ref=totals, send_sem=total_send.at[target],
            recv_sem=total_recv.at[0], device_id={"grp": target}, device_id_type=MESH,
        )

    @pl.when(me_g > 0)
    def _():
        to_root(me_g).start()

    high, low = halves(level)
    both = mm(jnp.concatenate([high, low], axis=0), nodal_v[...], 1, 1)
    level_out[...] = both[0:64] + both[64:128]
    every_owner.wait_send()

    @pl.when(me_g == 0)
    def _():
        pltpu.make_async_remote_copy(
            src_ref=gathered.at[pl.ds(1, n_grp - 1)], dst_ref=gathered.at[pl.ds(1, n_grp - 1)], send_sem=part_send.at[0],
            recv_sem=part_recv.at[0], device_id={"grp": 1}, device_id_type=MESH,
        ).wait_recv()
        sums = [parts[...]] + [gathered[k] for k in range(1, n_grp)]
        while len(sums) > 1:
            sums = [sums[k] + sums[k + 1] for k in range(0, len(sums), 2)]
        totals[...] = sums[0]
        for k in (1, 2, 15, 3, 4, 5, 6, 7):
            from_root(k).start()

    @pl.when(me_g > 0)
    def _():
        from_root(me_g).wait_recv()

    @pl.when(me_g == 15)
    def _():
        for k in HANDED:
            from_root(k).start()

    ends = totals[32:40, :]
    ends = jnp.concatenate([ends, pltpu.roll(ends, 64, 1)], axis=0)
    high, low = halves(jnp.concatenate([totals[0:16, :], totals[16:32, :], ends], axis=1))
    both = mm(jnp.concatenate([high, low], axis=0), nodal_v[...], 1, 1)
    coarse_out[...] = both[0:16] + both[16:32]

    @pl.when(me_g > 0)
    def _():
        to_root(me_g).wait_send()

    @pl.when(me_g == 0)
    def _():
        for k in (1, 2, 15, 3, 4, 5, 6, 7):
            from_root(k).wait_send()

    @pl.when(me_g == 15)
    def _():
        for k in HANDED:
            from_root(k).wait_send()


def body(n_grp, n_dev, elem_stiff, density, owner, agg_slot, par_octant, agg_octant, coarse_map):
    first, lift, signs, nodal = constants()
    row = lambda array: array.reshape(1, -1)
    args = (
        elem_stiff, row(density), row(owner), row(agg_slot), row(par_octant), row(agg_octant), row(coarse_map),
        jnp.asarray(first), jnp.asarray(lift), jnp.asarray(signs), jnp.asarray(nodal),
    )
    dma = pltpu.SemaphoreType.DMA
    level, coarse = pl.pallas_call(
        functools.partial(kernel, n_grp, n_dev),
        out_shape=(pltpu.VMEM((64, 576), F32), pltpu.VMEM((16, 576), F32)),
        in_specs=[pl.BlockSpec(memory_space=pltpu.HBM)] * len(args),
        out_specs=(pl.BlockSpec(memory_space=pltpu.VMEM), pl.BlockSpec(memory_space=pltpu.VMEM)),
        scratch_shapes=[pltpu.VMEM(a.shape, a.dtype) for a in args] + [
            pltpu.VMEM((8, 256, 512), BF16),
            pltpu.VMEM((n_dev, PACK, 128), F32),
            pltpu.VMEM((n_dev, PACK, 128), F32),
            pltpu.VMEM((PACK, 128), F32),
            pltpu.VMEM((n_grp, PACK, 128), F32),
            pltpu.VMEM((PACK, 128), F32),
            dma((9,)), dma((1,)), dma((2,)), dma((1,)), dma((1,)),
            dma((1,)), dma((1,)), dma((n_grp,)), dma((1,)),
        ],
        compiler_params=pltpu.CompilerParams(
            collective_id=0, has_side_effects=True, vmem_limit_bytes=63 * 1024 * 1024
        ),
    )(*args)
    return level.T, coarse.T


def solution(mesh):
    split = P(("grp", "dev"))
    return jax.shard_map(
        functools.partial(body, mesh.shape["grp"], mesh.shape["dev"]),
        mesh=mesh,
        in_specs=(P(None, ("grp", "dev")), split, P(("grp", "dev"), None), split, split, split, split),
        out_specs=(P(None, ("grp", "dev")), P(None, "dev")),
        check_vma=False,
    )
```

```python
import functools

import jax
import jax.numpy as jnp
import ml_dtypes
import numpy as np
from jax import lax
from jax.experimental import pallas as pl
from jax.experimental.pallas import tpu as pltpu
from jax.sharding import PartitionSpec as P

MESH = pl.DeviceIdType.MESH
F32, BF16 = jnp.float32, jnp.bfloat16
MODES = 300
CODE = 300
COLS = 304
WIDE = 384
KEEP = ((0, 384), (400, 432), (448, 480), (496, 528), (544, 576))
SLOTS = 16
FAR_FIRST = sorted(
    [(dx, dy, dc) for dx in range(4) for dy in range(4) for dc in range(2) if dx + dy + dc],
    key=lambda step: -(min(step[0], 4 - step[0]) + min(step[1], 4 - step[1])),
)
HANDED = (8, 9, 10, 11, 12, 13, 14)
PACK = 40


def prolong_np():
    table = np.zeros((8, 24, 24))
    for octant in range(8):
        for child in range(8):
            for corner in range(8):
                value = 1.0
                for bit in range(3):
                    place = (((octant >> bit) & 1) + ((child >> bit) & 1)) / 2.0
                    value *= place if (corner >> bit) & 1 else 1.0 - place
                for comp in range(3):
                    table[octant, child * 3 + comp, corner * 3 + comp] = value
    return table


def constants():
    table = prolong_np()
    axis = np.array([[1.0, -1.0], [1.0, 1.0]])
    basis = np.kron(np.kron(np.kron(axis, axis), axis), np.eye(3))
    pairs = [(k, l) for k in range(24) for l in range(k, 24)]
    ks, ls = np.array([p[0] for p in pairs]), np.array([p[1] for p in pairs])
    kept = np.concatenate([np.arange(a, b) for a, b in KEEP])
    row_i, row_j = kept // 24, kept % 24
    used = row_i <= row_j
    off = (row_i != row_j)[None, :]
    first = np.zeros((8, COLS, kept.size))
    for octant in range(8):
        modes = table[octant] @ basis
        term = modes[row_i][:, ks].T * modes[row_j][:, ls].T
        swap = modes[row_j][:, ks].T * modes[row_i][:, ls].T
        first[octant, :MODES] = np.where(used[None, :], term + off * swap, 0.0) / 64.0
    step = np.linalg.inv(basis) @ table[7] @ basis
    lift = np.zeros((WIDE, WIDE))
    lift[:MODES, :MODES] = step[ks][:, ks].T * step[ls][:, ls].T + (ks != ls)[None, :] * (step[ls][:, ks].T * step[ks][:, ls].T)
    signs = np.zeros((WIDE, 8))
    parity = (ks // 3) ^ (ls // 3)
    for octant in range(8):
        sign = np.ones(MODES)
        for bit in range(3):
            sign *= np.where((parity >> bit) & 1, 1.0 if (octant >> bit) & 1 else -1.0, 1.0)
        signs[:MODES, octant] = sign
    nodal = np.zeros((576, WIDE))
    a, b = np.arange(576) // 24, np.arange(576) % 24
    nodal[:, :MODES] = basis[a][:, ks] * basis[b][:, ls] + (ks != ls)[None, :] * basis[a][:, ls] * basis[b][:, ks]
    cast = lambda array: np.asarray(array).astype(ml_dtypes.bfloat16)
    return cast(first), cast(lift), cast(signs), cast(nodal)


def mm(left, right, left_dim=1, right_dim=0):
    return lax.dot_general(left, right, (((left_dim,), (right_dim,)), ((), ())), preferred_element_type=F32)


def iota(shape, dim):
    return lax.broadcasted_iota(jnp.int32, shape, dim)


def halves(value):
    high = value.astype(BF16)
    return high, (value - high.astype(F32)).astype(BF16)


def ones_where(mask):
    return jnp.where(mask, 1.0, 0.0).astype(BF16)


def kernel(
    n_grp, n_dev,
    stiff, dens, owner, slot, par_oct, agg_oct, agg_map, first, lift, signs, nodal,
    level_out, coarse_out,
    stiff_v, dens_v, owner_v, slot_v, par_oct_v, agg_oct_v, agg_map_v, first_v, lift_v, signs_v, nodal_v,
    xt, outgo, income, parts, gathered, totals,
    in_sem, first_sem, stiff_sem, send_sem, recv_sem, part_send, part_recv, total_send, total_recv,
):
    me_g, me_d = lax.axis_index("grp"), lax.axis_index("dev")
    blocks = 8

    small = [
        pltpu.make_async_copy(src, dst, in_sem.at[index])
        for index, (src, dst) in enumerate((
            (dens, dens_v), (owner, owner_v), (slot, slot_v), (par_oct, par_oct_v),
            (agg_oct, agg_oct_v), (agg_map, agg_map_v), (signs, signs_v),
        ))
    ]
    lift_load = pltpu.make_async_copy(lift, lift_v, in_sem.at[7])
    nodal_load = pltpu.make_async_copy(nodal, nodal_v, in_sem.at[8])
    first_load = pltpu.make_async_copy(first, first_v, first_sem.at[0])
    stiff_load = pltpu.make_async_copy(stiff, stiff_v, stiff_sem.at[0])
    for load in [stiff_load] + small + [first_load, lift_load, nodal_load]:
        load.start()

    barrier = pltpu.get_barrier_semaphore()

    def greet_dev(k, _):
        pl.semaphore_signal(barrier, inc=1, device_id={"dev": lax.rem(me_d + k, n_dev)}, device_id_type=MESH)
        return 0

    def greet_grp(k, _):
        pl.semaphore_signal(barrier, inc=1, device_id={"grp": k}, device_id_type=MESH)
        return 0

    lax.fori_loop(1, n_dev, greet_dev, 0)

    @pl.when(me_g == 0)
    def _():
        lax.fori_loop(1, n_grp, greet_grp, 0)

    @pl.when((me_g >= 8) & (me_g <= 14))
    def _():
        greet_grp(15, 0)

    @pl.when(((me_g >= 1) & (me_g <= 7)) | (me_g == 15))
    def _():
        greet_grp(0, 0)

    pos = iota((256, 256), 0)
    perm = ones_where(iota((256, 256), 1) == 8 * (pos % 32) + pos // 32)

    def turn(b):
        lanes = slice(256 * b, 256 * (b + 1))
        block = jnp.concatenate([stiff_v[a:z, lanes] for a, z in KEEP], axis=0)
        rows = mm(perm, block, 1, 1).astype(BF16)
        for o in range(8):
            xt[o, 32 * b:32 * (b + 1), :] = rows[32 * o:32 * (o + 1)]

    for load in [stiff_load] + small[:4] + small[6:]:
        load.wait()
    for b in range(8):
        turn(b)

    owner_row = owner_v[...]
    hits = iota((n_dev, 256), 0) == owner_row
    before = ones_where(iota((256, 256), 0) < iota((256, 256), 1))
    hits_f = jnp.where(hits, 1.0, 0.0)
    rank = jnp.sum(mm(hits_f.astype(BF16), before) * hits_f, axis=0, keepdims=True)
    place = owner_row * SLOTS + rank.astype(jnp.int32)
    code = slot_v[...].astype(F32) + 1.0

    picks = ones_where(iota((n_dev * SLOTS, 256), 0) == place)

    dens_row = dens_v[...]
    dens_8 = jnp.concatenate([dens_row[:, 256 * b:256 * (b + 1)] for b in range(blocks)], axis=0)
    weight = 0.001 + 0.999 * dens_8 * dens_8 * dens_8
    one = weight.astype(BF16)
    rest = weight - one.astype(F32)
    two = rest.astype(BF16)
    three = (rest - two.astype(F32)).astype(BF16)
    pieces = jnp.concatenate([one.astype(F32), two.astype(F32), three.astype(F32)], axis=0).astype(BF16)
    turned = mm(perm, pieces, 1, 1).astype(BF16)
    spread = ones_where(iota((24, 256), 0) % 8 == iota((24, 256), 1) // 32)
    spread_w = mm(turned, spread)
    own_row = iota((256, 256), 0) % 32 == iota((256, 256), 1) % 32
    weights = jnp.sum(jnp.where(own_row, spread_w, 0.0).reshape(8, 32, 256), axis=1)

    octs = ones_where(iota((8, 256), 0) == par_oct_v[...])
    flips = mm(signs_v[0:COLS, :], octs)

    first_load.wait()
    lift_load.wait()
    parent = None
    for o in range(8):
        term = mm(first_v[o], xt[o], 1, 1) * weights[o:o + 1, :]
        parent = term if parent is None else parent + term

    high, low = halves(parent * flips)
    lift_c = lift_v[0:COLS, :]
    gap = jnp.zeros((WIDE - COLS, 256), BF16)
    sent = mm(jnp.concatenate([lift_c, lift_c], axis=1), jnp.concatenate([high, gap, low, gap], axis=0)) * flips
    sent = jnp.where(iota((COLS, 256), 0) == CODE, code, sent)
    tail = sent[256:COLS]
    gap = jnp.zeros((16, 256), F32)
    full = jnp.concatenate([sent, gap, tail, gap], axis=0)
    high, low = halves(full)

    chosen = mm(jnp.concatenate([picks, picks], axis=1), jnp.concatenate([high, low], axis=1), 1, 1)
    outgo[:, 0:16, :] = chosen[:, 0:128].reshape(n_dev, 16, 128)
    outgo[:, 16:32, :] = chosen[:, 128:256].reshape(n_dev, 16, 128)
    ends = chosen[:, 256:384].reshape(n_dev, 2, 8, 128)
    outgo[:, 32:40, :] = jnp.where(iota((n_dev, 8, 128), 2) < 64, ends[:, 0], ends[:, 1])

    @pl.when((me_g == 0) | (me_g == 15))
    def _():
        pl.semaphore_wait(barrier, n_dev - 1 + 8)

    @pl.when((me_g >= 1) & (me_g <= 14))
    def _():
        pl.semaphore_wait(barrier, n_dev)

    def to_owner(peer):
        return pltpu.make_async_remote_copy(
            src_ref=outgo.at[peer], dst_ref=income.at[me_d], send_sem=send_sem.at[0],
            recv_sem=recv_sem.at[0], device_id={"dev": peer}, device_id_type=MESH,
        )

    every_owner = pltpu.make_async_remote_copy(
        src_ref=outgo.at[pl.ds(0, n_dev - 1)], dst_ref=income.at[pl.ds(0, n_dev - 1)], send_sem=send_sem.at[0],
        recv_sem=recv_sem.at[0], device_id={"dev": lax.rem(me_d + 1, n_dev)}, device_id_type=MESH,
    )

    x, y, core = lax.div(me_d, 8), lax.rem(lax.div(me_d, 2), 4), lax.rem(me_d, 2)
    for dx, dy, dc in FAR_FIRST:
        to_owner((lax.rem(x + dx, 4) * 4 + lax.rem(y + dy, 4)) * 2 + lax.rem(core + dc, 2)).start()
    income[me_d] = outgo[me_d]

    for load in small[4:6]:
        load.wait()
    octs = ones_where(iota((8, 64), 0) == agg_oct_v[...])
    agg_flips = mm(octs, signs_v[...], 0, 1)
    sums = ones_where(iota((16, 64), 0) == agg_map_v[...])
    nodal_load.wait()

    every_owner.wait_recv()

    lane = iota((8, 128), 1)
    code_at = ones_where(lane == CODE - 256 + 64 * iota((8, 128), 0))
    packed = income[:, 32:40, :].reshape(n_dev * 8, 128)
    codes = mm(code_at, packed.astype(BF16), 1, 1).astype(jnp.int32)
    level = []
    for h in range(2):
        into = ones_where(iota((64, n_dev * 8), 0) == codes[h:h + 1, :] - 1)
        wide = jnp.concatenate([
            income[:, 8 * h:8 * h + 8, :].reshape(n_dev * 8, 128),
            income[:, 16 + 8 * h:24 + 8 * h, :].reshape(n_dev * 8, 128),
            packed,
        ], axis=1)
        high, low = halves(wide)
        level.append(mm(jnp.concatenate([into, into], axis=1), jnp.concatenate([high, low], axis=0)))
    ends = level[0][:, 256:] + pltpu.roll(level[1][:, 256:], 64, 1)
    ends = jnp.where(iota((64, 128), 1) < MODES - 256, ends, 0.0)
    level = jnp.concatenate([level[0][:, :256] + level[1][:, :256], ends], axis=1)

    both = jnp.concatenate(halves(level * agg_flips), axis=0)
    lifted = mm(both, lift_v[...], 1, 1)
    high, low = halves((lifted[0:64] + lifted[64:128]) * agg_flips)
    share = mm(jnp.concatenate([sums, sums], axis=1), jnp.concatenate([high, low], axis=0))
    parts[0:16, :] = share[:, 0:128]
    parts[16:32, :] = share[:, 128:256]
    parts[32:40, :] = jnp.where(iota((8, 128), 1) < 64, share[0:8, 256:384], pltpu.roll(share[8:16, 256:384], 64, 1))

    def to_root(source):
        return pltpu.make_async_remote_copy(
            src_ref=parts, dst_ref=gathered.at[source], send_sem=part_send.at[0],
            recv_sem=part_recv.at[0], device_id={"grp": 0}, device_id_type=MESH,
        )

    def from_root(target):
        return pltpu.make_async_remote_copy(
            src_ref=totals, dst_ref=totals, send_sem=total_send.at[target],
            recv_sem=total_recv.at[0], device_id={"grp": target}, device_id_type=MESH,
        )

    @pl.when(me_g > 0)
    def _():
        to_root(me_g).start()

    high, low = halves(level)
    both = mm(jnp.concatenate([high, low], axis=0), nodal_v[...], 1, 1)
    level_out[...] = both[0:64] + both[64:128]
    every_owner.wait_send()

    @pl.when(me_g == 0)
    def _():
        pltpu.make_async_remote_copy(
            src_ref=gathered.at[pl.ds(1, n_grp - 1)], dst_ref=gathered.at[pl.ds(1, n_grp - 1)], send_sem=part_send.at[0],
            recv_sem=part_recv.at[0], device_id={"grp": 1}, device_id_type=MESH,
        ).wait_recv()
        sums = [parts[...]] + [gathered[k] for k in range(1, n_grp)]
        while len(sums) > 1:
            sums = [sums[k] + sums[k + 1] for k in range(0, len(sums), 2)]
        totals[...] = sums[0]
        for k in (1, 2, 15, 3, 4, 5, 6, 7):
            from_root(k).start()

    @pl.when(me_g > 0)
    def _():
        from_root(me_g).wait_recv()

    @pl.when(me_g == 15)
    def _():
        for k in HANDED:
            from_root(k).start()

    ends = totals[32:40, :]
    ends = jnp.concatenate([ends, pltpu.roll(ends, 64, 1)], axis=0)
    high, low = halves(jnp.concatenate([totals[0:16, :], totals[16:32, :], ends], axis=1))
    both = mm(jnp.concatenate([high, low], axis=0), nodal_v[...], 1, 1)
    coarse_out[...] = both[0:16] + both[16:32]

    @pl.when(me_g > 0)
    def _():
        to_root(me_g).wait_send()

    @pl.when(me_g == 0)
    def _():
        for k in (1, 2, 15, 3, 4, 5, 6, 7):
            from_root(k).wait_send()

    @pl.when(me_g == 15)
    def _():
        for k in HANDED:
            from_root(k).wait_send()


def body(n_grp, n_dev, elem_stiff, density, owner, agg_slot, par_octant, agg_octant, coarse_map):
    first, lift, signs, nodal = constants()
    row = lambda array: array.reshape(1, -1)
    args = (
        elem_stiff, row(density), row(owner), row(agg_slot), row(par_octant), row(agg_octant), row(coarse_map),
        jnp.asarray(first), jnp.asarray(lift), jnp.asarray(signs), jnp.asarray(nodal),
    )
    dma = pltpu.SemaphoreType.DMA
    level, coarse = pl.pallas_call(
        functools.partial(kernel, n_grp, n_dev),
        out_shape=(pltpu.VMEM((64, 576), F32), pltpu.VMEM((16, 576), F32)),
        in_specs=[pl.BlockSpec(memory_space=pltpu.HBM)] * len(args),
        out_specs=(pl.BlockSpec(memory_space=pltpu.VMEM), pl.BlockSpec(memory_space=pltpu.VMEM)),
        scratch_shapes=[pltpu.VMEM(a.shape, a.dtype) for a in args] + [
            pltpu.VMEM((8, 256, 512), BF16),
            pltpu.VMEM((n_dev, PACK, 128), F32),
            pltpu.VMEM((n_dev, PACK, 128), F32),
            pltpu.VMEM((PACK, 128), F32),
            pltpu.VMEM((n_grp, PACK, 128), F32),
            pltpu.VMEM((PACK, 128), F32),
            dma((9,)), dma((1,)), dma((1,)), dma((1,)), dma((1,)),
            dma((1,)), dma((1,)), dma((n_grp,)), dma((1,)),
        ],
        compiler_params=pltpu.CompilerParams(
            collective_id=0, has_side_effects=True, vmem_limit_bytes=63 * 1024 * 1024
        ),
    )(*args)
    return level.T, coarse.T


def solution(mesh):
    split = P(("grp", "dev"))
    return jax.shard_map(
        functools.partial(body, mesh.shape["grp"], mesh.shape["dev"]),
        mesh=mesh,
        in_specs=(P(None, ("grp", "dev")), split, P(("grp", "dev"), None), split, split, split, split),
        out_specs=(P(None, ("grp", "dev")), P(None, "dev")),
        check_vma=False,
    )
```
